32 devices in a mesh: section: 2 (over x), expert: 16 (over z, y, core).
Axes of the slice: x: 2, y: 2, z: 4, core: 2. Of those that a mesh axis runs over, the one named last changes fastest.
Arguments:
- in_flight: bfloat16 [2, 2, 512, 1024], P('section', None, 'expert'), may hold values from -6 to 6
- arriving: bfloat16 [1, 2, 512, 1024], P(None, None, 'expert'), may hold values from -6 to 6
- norm_gain: float32 [2, 1024], P('section'), may hold values from 0.1 to 1.9
- gate_up: bfloat16 [2, 16, 1024, 1536], P('section', 'expert'), may hold values from -0.1875 to 0.1875
- w_down: bfloat16 [2, 16, 768, 1024], P('section', 'expert'), may hold values from -0.21875 to 0.21875
- expert_ids: int32 [2, 2, 2, 512, 8], P(None, 'section', None, 'expert'), may hold values from 0 to 15, all different within a row; in each aligned block of 32 rows (0 to 31, 32 to 63, ..., all dimensions but the last counted through in order) at most 16 rows name the same one
- route_weights: float32 [2, 2, 2, 512, 8], P(None, 'section', None, 'expert'), may hold values from 0.05 to 1
Outputs:
- section_outputs: bfloat16 [2, 2, 2, 512, 1024], P(None, 'section', None, 'expert')
The draws below stay inside these ranges and needn't reach their ends.
Inputs may be any that keep to these rules, and one draw needn't show every extreme that they name: `expert_ids`: each token names 8 different experts. In each micro-batch of each step and section, the tokens of one aligned block of 32 (the rows of one device) name one expert at most 16 times.
All inputs are finite; a program needn't handle non-finite values.
Results may differ from the reference program's by a relative error of at most 0.007.
Values may be sent and summed in bfloat16 or wider, within the bound.
No kernel may reach another device: no remote copies, remote signals or barrier semaphores. Data moves between devices by JAX's collectives and lax.ppermute only.
A program may use at most 64 MiB of HBM per device.

```python
import math
import jax
import jax.numpy as jnp
import numpy as np
from jax import lax

D = 1024
FF = 768
TOPK = 8
MICRO = 2
TICKS = 2
MB_TOK = 32
EXPERTS = 16
TOKENS_MB = 512
CAP = 16
N_SECTION = 2


def steps_of(stream_key, shape, cuts, smallest, high):
    loudness, own = 1.0, jax.random.fold_in(stream_key, 6)
    for position, shards_of in cuts:
        heights = jnp.exp(jax.random.uniform(jax.random.fold_in(own, position), (shards_of,), jnp.float32, smallest / len(cuts), high / len(cuts)))
        loudness = loudness * jnp.repeat(heights, shape[position] // shards_of).reshape([-1 if axis == position else 1 for axis in range(len(shape))])
    return loudness


def assign_block(own_key, own, number, rows, amount, top, limit, lean):
    sequence = jax.random.permutation(own_key, amount)
    heavy_load, common = portions_of(amount, rows * top, limit, lean, True), portions_of(amount, rows * top, limit, lean, False)
    places = jnp.arange(amount)

    def named(sizes, turn):
        used = int((sizes > 0).sum())
        fixed = max(1, used // 4)
        shifted = fixed + (places - fixed + turn * (used - fixed)) % max(1, amount - fixed)
        return jnp.zeros((amount,), jnp.int32).at[sequence[jnp.where(places < fixed, places, shifted)]].set(jnp.asarray(sizes, jnp.int32))

    sizes = jnp.where(number % 4 == 0, named(heavy_load, number // 4), named(common, number - number // 4 - 1))
    mixed = jax.random.permutation(jax.random.fold_in(own, 3), amount)
    donor, taker = mixed[0:amount // 2 * 2:2], mixed[1:amount // 2 * 2:2]
    margin = jnp.minimum(sizes[donor] - 1, limit - sizes[taker]) // 2
    margin = jnp.where((donor == sequence[0]) | (taker == sequence[0]) | (sizes[taker] == 0), 0, jnp.maximum(margin, 0))
    shifted = jax.random.randint(jax.random.fold_in(own, 4), (amount // 2,), 0, 1 << 20) % (margin + 1)
    sizes = sizes.at[donor].add(-shifted).at[taker].add(shifted)
    items = jnp.searchsorted(jnp.cumsum(sizes), jnp.arange(rows * top), side="right").astype(jnp.int32)
    grid = items.reshape(top, rows).T
    grid = grid[jax.random.permutation(jax.random.fold_in(own, 1), rows)]
    turn = jax.random.randint(jax.random.fold_in(own, 2), (rows, 1), 0, top)
    return jnp.take_along_axis(grid, (jnp.arange(top)[None, :] + turn) % top, axis=1)


def portions_of(count, total, reach, slope, full):
    loads = [(1 << 20) // math.isqrt(grade ** slope) + 1 for grade in range(1, count + 1)]
    largest = reach if full else min(reach, max(-(-total // count), total * loads[0] // sum(loads)))
    least = 1 if total - largest >= count - 1 else 0
    counts, spare = [largest] + [least] * (count - 1), total - largest - least * (count - 1)
    while spare > 0:
        candidates = [i for i in range(1, count) if counts[i] < largest] or [i for i in range(1, count) if counts[i] < reach]
        mass, budget = sum([loads[i] for i in candidates]), spare
        for i in candidates:
            extra = min(reach - counts[i], max(1, budget * loads[i] // mass), spare)
            counts[i] = counts[i] + extra
            spare = spare - extra
    return np.array(counts)


def scatter_about(key, shape, deviation, reach, split=(), kind=jnp.bfloat16):
    entries = jax.random.normal(key, shape, jnp.float32) * deviation
    if len(split) > 0:
        entries = steps_of(key, shape, split, -0.22, 0.18) * entries
    return jnp.clip(entries, min=-reach, max=reach).astype(kind)


def setup_inputs(seed: int = 0) -> dict:
    streams_of = jax.random.split(jax.random.key(seed), 8)
    in_flight = scatter_about(streams_of[0], (N_SECTION, MICRO, TOKENS_MB, D), 1.0, 6.0, ((0, 2), (2, 16)))
    arriving = scatter_about(streams_of[1], (TICKS - 1, MICRO, TOKENS_MB, D), 1.0, 6.0, ((2, 16),))
    norm_gain = jnp.clip(1.0 + 0.18 * jax.random.normal(streams_of[2], (N_SECTION, D), jnp.float32), 0.1, 1.9)
    gate_up = scatter_about(streams_of[3], (N_SECTION, EXPERTS, D, 2 * FF), D ** -0.5, 0.1875, ((0, 2), (1, 16)))
    w_down = scatter_about(streams_of[4], (N_SECTION, EXPERTS, FF, D), FF ** -0.5, 0.21875, ((0, 2), (1, 16)))
    expert_ids_keys = jax.random.split(jax.random.fold_in(streams_of[5], 1), TICKS * N_SECTION * MICRO * TOKENS_MB // MB_TOK)
    expert_ids_turns = jax.random.permutation(jax.random.fold_in(streams_of[5], 3), TICKS * N_SECTION * MICRO * TOKENS_MB // MB_TOK)
    expert_ids = jax.vmap(lambda own, number: assign_block(jax.random.fold_in(streams_of[5], 2), own, number, MB_TOK, EXPERTS, TOPK, CAP, 2))(expert_ids_keys, expert_ids_turns).reshape((TICKS, N_SECTION, MICRO, TOKENS_MB, TOPK))
    route_weights = jnp.clip(jnp.exp(math.log(1.0) - 2.9957323 * jax.random.uniform(streams_of[6], (TICKS, N_SECTION, MICRO, TOKENS_MB, TOPK), jnp.float32) ** steps_of(streams_of[6], (TICKS, N_SECTION, MICRO, TOKENS_MB, TOPK), ((1, 2), (3, 16)), -0.2, 0.2)), 0.05, 1.0)
    return dict(in_flight=in_flight, arriving=arriving, norm_gain=norm_gain, gate_up=gate_up, w_down=w_down, expert_ids=expert_ids, route_weights=route_weights)


def moe_layer(inflow, gain_row, gate_proj, down_proj, choice_ids, choice_weights):
    widened = inflow.astype(jnp.float32)
    inverse_rms = lax.rsqrt(lax.optimization_barrier(jnp.mean(widened * widened, axis=-1, keepdims=True)) + 1e-06)
    normed = (widened * inverse_rms * gain_row[None, :].astype(jnp.float32)).astype(jnp.bfloat16)
    blocks = TOKENS_MB // MB_TOK
    flat_ids = choice_ids.reshape(blocks, MB_TOK * TOPK).astype(jnp.int32)
    onehot = (flat_ids[:, :, None] == jnp.arange(EXPERTS, dtype=jnp.int32)[None, None, :]).astype(jnp.int32)
    earlier = jnp.cumsum(onehot, axis=1) - onehot
    slot_of = lax.optimization_barrier(jnp.sum(earlier * onehot, axis=-1)).astype(jnp.int32)
    row_index = (jnp.arange(blocks, dtype=jnp.int32)[:, None] * CAP + slot_of).reshape(-1)
    chosen = flat_ids.reshape(-1)
    token_index = jnp.arange(TOKENS_MB * TOPK, dtype=jnp.int32) // TOPK
    buffer = jnp.zeros((EXPERTS, blocks * CAP, D), jnp.bfloat16).at[chosen, row_index].set(normed[token_index])

    def one_expert(pieces):
        rows_in, w_in, w_out = pieces
        projected = jnp.dot(rows_in, w_in, preferred_element_type=jnp.float32)
        hidden = (jax.nn.silu(projected[:, :FF]) * projected[:, FF:]).astype(jnp.bfloat16)
        return jnp.dot(hidden, w_out, preferred_element_type=jnp.float32).astype(jnp.bfloat16)
    expert_out = lax.map(one_expert, (buffer, gate_proj, down_proj))
    picked = expert_out[chosen, row_index].reshape(TOKENS_MB, TOPK, D).astype(jnp.float32)
    branch = lax.optimization_barrier(jnp.sum(picked * choice_weights.astype(jnp.float32)[:, :, None], axis=1))
    return (widened + branch).astype(jnp.bfloat16)

def reference(in_flight, arriving, norm_gain, gate_up, w_down, expert_ids, route_weights):
    results = []
    inflow = in_flight
    for step_number in range(TICKS):
        if step_number > 0:
            inflow = jnp.concatenate([arriving[step_number - 1][None], results[-1][:-1]], axis=0)

        def one_section(pieces):
            section_in, gain_row, gate_proj, down_proj, section_ids, section_weights = pieces
            return jnp.stack([moe_layer(section_in[index], gain_row, gate_proj, down_proj, section_ids[index], section_weights[index]) for index in range(MICRO)])
        results.append(lax.map(one_section, (inflow, norm_gain, gate_up, w_down, expert_ids[step_number], route_weights[step_number])))
    return jnp.stack(results)
```

```python
import functools

import jax
import jax.numpy as jnp
from jax import lax
from jax.experimental import pallas as pl
from jax.experimental.pallas import tpu as pltpu
from jax.sharding import PartitionSpec as P

LANES = 128


def normalize(inflow, gain_row):
    widened = inflow.astype(jnp.float32)
    inverse_rms = lax.rsqrt(jnp.mean(widened * widened, axis=-1, keepdims=True) + 1e-06)
    return (widened * inverse_rms * gain_row).astype(jnp.bfloat16)


def first_kernel(
    experts_all, inflow_hbm, gain_hbm, ids_hbm, weights_hbm, *refs
):
    inflow, gain, ids, weights, sem = refs[-5:]
    payloads, later = refs[:-6], refs[-6]
    copies = [
        pltpu.make_async_copy(source, target, sem.at[number])
        for number, (source, target) in enumerate(
            ((ids_hbm, ids), (weights_hbm, weights), (inflow_hbm, inflow), (gain_hbm, gain))
        )
    ]
    for copy in copies:
        copy.start()
    for copy in copies:
        copy.wait()
    steps, micro_count, top_count, tokens = ids.shape
    features = inflow.shape[-1]
    width = later.shape[-1]
    expert = lax.broadcasted_iota(jnp.int32, (experts_all, tokens), 0)
    columns = []
    for step in range(steps):
        for micro in range(micro_count):
            dense = jnp.zeros((experts_all, tokens), jnp.float32)
            for k in range(top_count):
                named = ids[step, micro, k : k + 1, :] == expert
                dense = dense + jnp.where(named, weights[step, micro, k : k + 1, :], 0.0)
            high = dense.astype(jnp.bfloat16).astype(jnp.float32)
            empty = jnp.zeros((width - 2 * experts_all, tokens), jnp.float32)
            columns.append(jnp.concatenate([high, dense - high, empty], axis=0))
    tails = jnp.concatenate(columns, axis=1).T.astype(jnp.bfloat16)
    tails = tails.reshape(steps, micro_count, tokens, width)
    for micro, payload in enumerate(payloads):
        payload[:, :features] = normalize(inflow[micro], gain[...])
        payload[:, features:] = tails[0, micro]
    later[...] = tails[1:]


def first_payload(inflow, gain, ids, weights, experts_all):
    micro_count, tokens, features = inflow.shape
    steps = ids.shape[0]
    width = -(-2 * experts_all // LANES) * LANES
    return pl.pallas_call(
        functools.partial(first_kernel, experts_all),
        out_shape=(jax.ShapeDtypeStruct((tokens, features + width), jnp.bfloat16),) * micro_count
        + (jax.ShapeDtypeStruct((steps - 1, micro_count, tokens, width), jnp.bfloat16),),
        in_specs=[pl.BlockSpec(memory_space=pltpu.HBM)] * 4,
        out_specs=[pl.BlockSpec(memory_space=pltpu.VMEM)] * (micro_count + 1),
        scratch_shapes=[
            pltpu.VMEM(inflow.shape, inflow.dtype),
            pltpu.VMEM(gain.shape, gain.dtype),
            pltpu.VMEM(ids.shape, ids.dtype),
            pltpu.VMEM(weights.shape, weights.dtype),
            pltpu.SemaphoreType.DMA((4,)),
        ],
        compiler_params=pltpu.CompilerParams(vmem_limit_bytes=8 * 1024 * 1024),
        name="first_payload",
    )(inflow, gain, ids, weights)


def leave_kernel(step, micro, inflow, own, *refs):
    parts, (fresh, gain, tail, out, leaving, payload) = refs[:-6], refs[-6:]
    features = inflow.shape[-1]
    total = inflow[...].reshape(own.shape).astype(jnp.float32) + own[...]
    for part in parts:
        total = total + part[...].astype(jnp.float32)
    result = total.astype(jnp.bfloat16)
    out[...] = result
    is_last = lax.axis_index("section") == lax.axis_size("section") - 1
    arrived = fresh[step, micro].astype(jnp.float32)
    gone = jnp.where(is_last, arrived, result.astype(jnp.float32))
    leaving[...] = gone.astype(jnp.bfloat16)
    payload[:, :features] = normalize(gone, gain[...])
    payload[:, features:] = tail[step, micro]


def leave(step, micro, inflow, own, parts, fresh, gain, tail):
    tokens, features = own.shape
    whole = pl.BlockSpec(memory_space=pltpu.VMEM)
    rows = jax.ShapeDtypeStruct((tokens, features), jnp.bfloat16)
    return pl.pallas_call(
        functools.partial(leave_kernel, step, micro),
        out_shape=(
            rows,
            rows,
            jax.ShapeDtypeStruct((tokens, features + tail.shape[-1]), jnp.bfloat16),
        ),
        in_specs=[whole] * (5 + len(parts)),
        out_specs=[whole] * 3,
        compiler_params=pltpu.CompilerParams(vmem_limit_bytes=8 * 1024 * 1024),
        name="leave",
    )(inflow, own, *parts, fresh, gain, tail)


def swap_core(value):
    size = lax.axis_size("expert")
    return lax.ppermute(value, "expert", [(i, i ^ 1) for i in range(size)])


def swap_inner(value):
    size = lax.axis_size("expert")
    return lax.ppermute(value, "expert", [(i, i ^ 2) for i in range(size)])


def rotate_outer(value, by):
    size = lax.axis_size("expert")
    return lax.ppermute(value, "expert", [(i, (i + 4 * by) % size) for i in range(size)])


def next_section(value, by):
    sections, size = lax.axis_size("section"), lax.axis_size("expert")
    pairs = [
        (s * size + i, (s + 1) % sections * size + (i + 4 * by) % size)
        for s in range(sections)
        for i in range(size)
    ]
    return lax.ppermute(value, ("section", "expert"), pairs)


def previous_section(value):
    sections = lax.axis_size("section")
    return lax.ppermute(value, "section", [(s, (s - 1) % sections) for s in range(sections)])


def serve_kernel(
    features, hidden_count, chunk, experts_all, local_count,
    near, far, own_in, far_in, own_out, far_out,
    near_sum, far_sum, rows, hidden,
):
    blocks, tokens = near.shape[:2]
    half = blocks * tokens
    rows[pl.ds(0, half)] = near[:, :, :features].reshape(half, features)
    rows[pl.ds(half, half)] = far[:, :, :features].reshape(half, features)
    tail = jnp.concatenate(
        [part[:, :, features:].reshape(half, -1) for part in (near, far)]
    ).astype(jnp.float32)
    lane = lax.broadcasted_iota(jnp.int32, tail.shape, 1)
    me = lax.axis_index("expert")
    total = None
    for side, (w_in, w_out) in enumerate(((own_in, own_out), (far_in, far_out))):
        for own in range(local_count):
            which = (me + side * (1 - 2 * (me % 2))) * local_count + own
            chosen = (lane == which) | (lane == which + experts_all)
            weight = jnp.sum(jnp.where(chosen, tail, 0.0), axis=-1, keepdims=True)
            for at in range(0, hidden_count, chunk):
                gate = jnp.dot(
                    rows[...], w_in[own, :, pl.ds(at, chunk)], preferred_element_type=jnp.float32
                )
                up = jnp.dot(
                    rows[...],
                    w_in[own, :, pl.ds(hidden_count + at, chunk)],
                    preferred_element_type=jnp.float32,
                )
                value = gate / (1.0 + jnp.exp(-gate)) * up * weight
                hidden[:, pl.ds(at, chunk)] = value.astype(jnp.bfloat16)
            out = jnp.dot(hidden[...], w_out[own], preferred_element_type=jnp.float32)
            total = out if total is None else total + out
    near_sum[...] = total[:half].reshape(near_sum.shape)
    far_sum[...] = total[half:].astype(jnp.bfloat16).reshape(far_sum.shape)


def serve(near, far, own_in, far_in, own_out, far_out, experts_all):
    blocks, tokens, width = near.shape
    local_count, features, _ = own_in.shape
    hidden_count = own_out.shape[1]
    chunk = 256 if hidden_count % 256 == 0 else hidden_count
    rows_all = 2 * blocks * tokens
    held = 2 * (own_in.size + own_out.size) * 2
    whole = pl.BlockSpec(memory_space=pltpu.VMEM)
    return pl.pallas_call(
        functools.partial(
            serve_kernel, features, hidden_count, chunk, experts_all, local_count
        ),
        out_shape=(
            jax.ShapeDtypeStruct((blocks, tokens, features), jnp.float32),
            jax.ShapeDtypeStruct((blocks, tokens, features), jnp.bfloat16),
        ),
        in_specs=[whole] * 6,
        out_specs=[whole] * 2,
        scratch_shapes=[
            pltpu.VMEM((rows_all, features), jnp.bfloat16),
            pltpu.VMEM((rows_all, hidden_count), jnp.bfloat16),
        ],
        compiler_params=pltpu.CompilerParams(vmem_limit_bytes=held + 8 * 1024 * 1024),
        cost_estimate=pl.CostEstimate(
            flops=2 * rows_all * 2 * local_count * 3 * features * hidden_count,
            bytes_accessed=held,
            transcendentals=rows_all * 2 * local_count * hidden_count,
        ),
        name="serve",
    )(near, far, own_in, far_in, own_out, far_out)


def local(in_flight, arriving, norm_gain, gate_up, w_down, expert_ids, route_weights):
    owners = lax.axis_size("expert")
    outer = owners // 4
    local_count = gate_up.shape[1]
    experts_all = owners * local_count
    steps = expert_ids.shape[0]
    micro_count = in_flight.shape[1]
    own_in, own_out = gate_up[0], w_down[0]
    far_in, far_out = swap_core(own_in), swap_core(own_out)
    *payloads, tails = first_payload(
        in_flight[0],
        norm_gain,
        jnp.swapaxes(expert_ids[:, 0], -1, -2),
        jnp.swapaxes(route_weights[:, 0], -1, -2),
        experts_all,
    )
    later_gain = previous_section(norm_gain)
    later_tails = previous_section(tails)
    inflows = [in_flight[0, micro] for micro in range(micro_count)]
    outputs = []
    for step in range(steps):
        results = []
        for micro in range(micro_count):
            payload, inflow = payloads[micro], inflows[micro]
            if step == 0:
                near = jnp.stack([payload] + [rotate_outer(payload, by) for by in range(1, outer)])
            else:
                near = jnp.stack([next_section(payload, by) for by in range(outer)])
            far = swap_inner(near)
            near_sum, far_sum = serve(near, far, own_in, far_in, own_out, far_out, experts_all)
            served = near_sum + swap_inner(far_sum).astype(jnp.float32)
            parts = [
                rotate_outer(served[by].astype(jnp.bfloat16), -by) for by in range(1, outer)
            ]
            if step < steps - 1:
                result, leaving, payloads[micro] = leave(
                    step, micro, inflow, served[0], parts, arriving, later_gain, later_tails
                )
                inflows[micro] = next_section(leaving, 0)
            else:
                total = inflow.astype(jnp.float32) + served[0]
                for part in parts:
                    total = total + part.astype(jnp.float32)
                result = total.astype(jnp.bfloat16)
            results.append(result)
        outputs.append(jnp.stack(results))
    return jnp.stack(outputs)[:, None]


def solution(mesh):
    return jax.shard_map(
        local,
        mesh=mesh,
        in_specs=(
            P("section", None, "expert", None),
            P(None, None, "expert", None),
            P("section", None),
            P("section", "expert", None, None),
            P("section", "expert", None, None),
            P(None, "section", None, "expert", None),
            P(None, "section", None, "expert", None),
        ),
        out_specs=P(None, "section", None, "expert", None),
        check_vma=False,
    )
```

```python
import functools

import jax
import jax.numpy as jnp
from jax import lax
from jax.experimental import pallas as pl
from jax.experimental.pallas import tpu as pltpu
from jax.sharding import PartitionSpec as P

LANES = 128


def normalize(inflow, gain_row):
    widened = inflow.astype(jnp.float32)
    inverse_rms = lax.rsqrt(jnp.mean(widened * widened, axis=-1, keepdims=True) + 1e-06)
    return (widened * inverse_rms * gain_row).astype(jnp.bfloat16)


def token_weights(experts_all, width, ids, weights):
    steps, micro_count, top_count, tokens = ids.shape
    expert = lax.broadcasted_iota(jnp.int32, (experts_all, tokens), 0)
    columns = []
    for step in range(steps):
        for micro in range(micro_count):
            dense = jnp.zeros((experts_all, tokens), jnp.float32)
            for k in range(top_count):
                named = ids[step, micro, k : k + 1, :] == expert
                dense = dense + jnp.where(named, weights[step, micro, k : k + 1, :], 0.0)
            high = dense.astype(jnp.bfloat16).astype(jnp.float32)
            empty = jnp.zeros((width - 2 * experts_all, tokens), jnp.float32)
            columns.append(jnp.concatenate([high, dense - high, empty], axis=0))
    tails = jnp.concatenate(columns, axis=1).T.astype(jnp.bfloat16)
    return tails.reshape(steps, micro_count, tokens, width)


def first_kernel(
    experts_all, inflow_hbm, gain_hbm, ids_hbm, weights_hbm, *refs
):
    payloads, (inflow, gain, ids, weights, sem) = refs[:-5], refs[-5:]
    copies = [
        pltpu.make_async_copy(source, target, sem.at[number])
        for number, (source, target) in enumerate(
            (
                (ids_hbm.at[pl.ds(0, 1)], ids),
                (weights_hbm.at[pl.ds(0, 1)], weights),
                (inflow_hbm, inflow),
                (gain_hbm, gain),
            )
        )
    ]
    for copy in copies:
        copy.start()
    for copy in copies:
        copy.wait()
    features = inflow.shape[-1]
    width = payloads[0].shape[-1] - features
    tails = token_weights(experts_all, width, ids, weights)
    for micro, payload in enumerate(payloads):
        payload[:, :features] = normalize(inflow[micro], gain[...])
        payload[:, features:] = tails[0, micro]


def first_payload(inflow, gain, ids, weights, experts_all, width):
    micro_count, tokens, features = inflow.shape
    return pl.pallas_call(
        functools.partial(first_kernel, experts_all),
        out_shape=(jax.ShapeDtypeStruct((tokens, features + width), jnp.bfloat16),) * micro_count,
        in_specs=[pl.BlockSpec(memory_space=pltpu.HBM)] * 4,
        out_specs=[pl.BlockSpec(memory_space=pltpu.VMEM)] * micro_count,
        scratch_shapes=[
            pltpu.VMEM(inflow.shape, inflow.dtype),
            pltpu.VMEM(gain.shape, gain.dtype),
            pltpu.VMEM((1,) + ids.shape[1:], ids.dtype),
            pltpu.VMEM((1,) + weights.shape[1:], weights.dtype),
            pltpu.SemaphoreType.DMA((4,)),
        ],
        compiler_params=pltpu.CompilerParams(vmem_limit_bytes=60 * 1024 * 1024),
        name="first_payload",
    )(inflow, gain, ids, weights)


def later_kernel(experts_all, after, own_in, own_out, ids, weights, gain, later):
    del after, own_in, own_out
    steps, micro_count, _, tokens = ids.shape
    made = token_weights(experts_all, later.shape[-1], ids, weights)[1:]
    at = (steps - 1) * micro_count * tokens
    later[:at] = made.reshape(at, later.shape[-1])
    width = later.shape[-1]
    pieces = gain.shape[-1] // width
    rest = jnp.concatenate(
        [gain[:, piece * width : (piece + 1) * width] for piece in range(pieces)], axis=0
    )
    for part in range(3):
        rounded = rest.astype(jnp.bfloat16)
        later[at + part * pieces : at + (part + 1) * pieces] = rounded
        rest = rest - rounded.astype(jnp.float32)


def later_rows(after, own_in, own_out, ids, weights, gain, experts_all, width):
    steps, micro_count, _, tokens = ids.shape
    rows = (steps - 1) * micro_count * tokens + 3 * gain.shape[-1] // width
    whole = pl.BlockSpec(memory_space=pltpu.VMEM)
    return pl.pallas_call(
        functools.partial(later_kernel, experts_all),
        out_shape=jax.ShapeDtypeStruct((rows, width), jnp.bfloat16),
        in_specs=[pl.BlockSpec(memory_space=pl.ANY)] + [whole] * 5,
        out_specs=whole,
        compiler_params=pltpu.CompilerParams(
            vmem_limit_bytes=2 * (own_in.size + own_out.size) + 8 * 1024 * 1024
        ),
        name="later_rows",
    )(after, own_in, own_out, ids, weights, gain)


def leave_kernel(step, micro, inflow, own, *refs):
    parts, (fresh, later, out, leaving, payload) = refs[:-5], refs[-5:]
    tokens, features = own.shape
    width = later.shape[-1]
    micro_count = fresh.shape[1]
    total = inflow[...].reshape(own.shape).astype(jnp.float32) + own[...]
    for part in parts:
        total = total + part[...].astype(jnp.float32)
    result = total.astype(jnp.bfloat16)
    out[...] = result
    is_last = lax.axis_index("section") == lax.axis_size("section") - 1
    arrived = fresh[step, micro].astype(jnp.float32)
    gone = jnp.where(is_last, arrived, result.astype(jnp.float32))
    leaving[...] = gone.astype(jnp.bfloat16)
    pieces = features // width
    at = later.shape[0] - 3 * pieces
    parts = [
        later[at + part * pieces : at + (part + 1) * pieces].astype(jnp.float32)
        for part in range(3)
    ]
    gain = parts[0] + parts[1] + parts[2]
    gain = jnp.concatenate([gain[piece : piece + 1] for piece in range(pieces)], axis=1)
    payload[:, :features] = normalize(gone, gain)
    first = (step * micro_count + micro) * tokens
    payload[:, features:] = later[first : first + tokens]


def leave(step, micro, inflow, own, parts, fresh, later):
    tokens, features = own.shape
    whole = pl.BlockSpec(memory_space=pltpu.VMEM)
    rows = jax.ShapeDtypeStruct((tokens, features), jnp.bfloat16)
    return pl.pallas_call(
        functools.partial(leave_kernel, step, micro),
        out_shape=(
            rows,
            rows,
            jax.ShapeDtypeStruct((tokens, features + later.shape[-1]), jnp.bfloat16),
        ),
        in_specs=[whole] * (4 + len(parts)),
        out_specs=[whole] * 3,
        compiler_params=pltpu.CompilerParams(vmem_limit_bytes=8 * 1024 * 1024),
        name="leave",
    )(inflow, own, *parts, fresh, later)


def swap_core(value):
    size = lax.axis_size("expert")
    return lax.ppermute(value, "expert", [(i, i ^ 1) for i in range(size)])


def swap_inner(value):
    size = lax.axis_size("expert")
    return lax.ppermute(value, "expert", [(i, i ^ 2) for i in range(size)])


def swap_outer(value, by):
    size = lax.axis_size("expert")
    return lax.ppermute(value, "expert", [(i, i ^ 4 * by) for i in range(size)])


def next_section(value, by):
    sections, size = lax.axis_size("section"), lax.axis_size("expert")
    pairs = [
        (s * size + i, (s + 1) % sections * size + (i ^ 4 * by))
        for s in range(sections)
        for i in range(size)
    ]
    return lax.ppermute(value, ("section", "expert"), pairs)


def previous_section(value):
    sections = lax.axis_size("section")
    return lax.ppermute(value, "section", [(s, (s - 1) % sections) for s in range(sections)])


def serve_kernel(
    features, hidden_count, chunk, experts_all, local_count,
    near, far, own_in, far_in, own_out, far_out,
    near_sum, far_sum, rows, hidden,
):
    blocks, tokens = near.shape[:2]
    half = blocks * tokens
    rows[pl.ds(0, half)] = near[:, :, :features].reshape(half, features)
    rows[pl.ds(half, half)] = far[:, :, :features].reshape(half, features)
    tail = jnp.concatenate(
        [part[:, :, features:].reshape(half, -1) for part in (near, far)]
    ).astype(jnp.float32)
    lane = lax.broadcasted_iota(jnp.int32, tail.shape, 1)
    me = lax.axis_index("expert")
    total = None
    for side, (w_in, w_out) in enumerate(((own_in, own_out), (far_in, far_out))):
        for own in range(local_count):
            which = (me + side * (1 - 2 * (me % 2))) * local_count + own
            chosen = (lane == which) | (lane == which + experts_all)
            weight = jnp.sum(jnp.where(chosen, tail, 0.0), axis=-1, keepdims=True)
            for at in range(0, hidden_count, chunk):
                gate = jnp.dot(
                    rows[...], w_in[own, :, pl.ds(at, chunk)], preferred_element_type=jnp.float32
                )
                up = jnp.dot(
                    rows[...],
                    w_in[own, :, pl.ds(hidden_count + at, chunk)],
                    preferred_element_type=jnp.float32,
                )
                value = gate / (1.0 + jnp.exp(-gate)) * up * weight
                hidden[:, pl.ds(at, chunk)] = value.astype(jnp.bfloat16)
            out = jnp.dot(hidden[...], w_out[own], preferred_element_type=jnp.float32)
            total = out if total is None else total + out
    near_sum[...] = total[:half].reshape(near_sum.shape)
    far_sum[...] = total[half:].astype(jnp.bfloat16).reshape(far_sum.shape)


def serve(near, far, own_in, far_in, own_out, far_out, experts_all):
    blocks, tokens, width = near.shape
    local_count, features, _ = own_in.shape
    hidden_count = own_out.shape[1]
    chunk = 256 if hidden_count % 256 == 0 else hidden_count
    rows_all = 2 * blocks * tokens
    held = 2 * (own_in.size + own_out.size) * 2
    whole = pl.BlockSpec(memory_space=pltpu.VMEM)
    return pl.pallas_call(
        functools.partial(
            serve_kernel, features, hidden_count, chunk, experts_all, local_count
        ),
        out_shape=(
            jax.ShapeDtypeStruct((blocks, tokens, features), jnp.float32),
            jax.ShapeDtypeStruct((blocks, tokens, features), jnp.bfloat16),
        ),
        in_specs=[whole] * 6,
        out_specs=[whole] * 2,
        scratch_shapes=[
            pltpu.VMEM((rows_all, features), jnp.bfloat16),
            pltpu.VMEM((rows_all, hidden_count), jnp.bfloat16),
        ],
        compiler_params=pltpu.CompilerParams(vmem_limit_bytes=held + 8 * 1024 * 1024),
        cost_estimate=pl.CostEstimate(
            flops=2 * rows_all * 2 * local_count * 3 * features * hidden_count,
            bytes_accessed=held,
            transcendentals=rows_all * 2 * local_count * hidden_count,
        ),
        name="serve",
    )(near, far, own_in, far_in, own_out, far_out)


def local(in_flight, arriving, norm_gain, gate_up, w_down, expert_ids, route_weights):
    owners = lax.axis_size("expert")
    outer = owners // 4
    local_count = gate_up.shape[1]
    experts_all = owners * local_count
    steps = expert_ids.shape[0]
    micro_count = in_flight.shape[1]
    width = -(-2 * experts_all // LANES) * LANES
    ids = jnp.swapaxes(expert_ids[:, 0], -1, -2)
    weights = jnp.swapaxes(route_weights[:, 0], -1, -2)
    payloads = first_payload(in_flight[0], norm_gain, ids, weights, experts_all, width)
    *payloads, gate_up, w_down = lax.optimization_barrier((*payloads, gate_up, w_down))
    own_in, own_out = gate_up[0], w_down[0]
    far_in, far_out = swap_core(own_in), swap_core(own_out)
    later = later_rows(
        payloads[0], own_in, own_out, ids, weights, norm_gain, experts_all, width
    )
    later = previous_section(later)
    inflows = [in_flight[0, micro] for micro in range(micro_count)]
    outputs = []
    for step in range(steps):
        results = []
        for micro in range(micro_count):
            payload, inflow = payloads[micro], inflows[micro]
            if step == 0:
                near = jnp.stack([payload] + [swap_outer(payload, by) for by in range(1, outer)])
                if micro == micro_count - 1:
                    near, far_in, far_out = lax.optimization_barrier((near, far_in, far_out))
            else:
                near = jnp.stack([next_section(payload, by) for by in range(outer)])
            far = swap_inner(near)
            if step > 0:
                far, inflow = lax.optimization_barrier((far, inflow))
            near_sum, far_sum = serve(near, far, own_in, far_in, own_out, far_out, experts_all)
            returned = swap_inner(far_sum)
            if step == 0 and micro == 0:
                returned, later = lax.optimization_barrier((returned, later))
            served = near_sum + returned.astype(jnp.float32)
            parts = [swap_outer(served[by].astype(jnp.bfloat16), by) for by in range(1, outer)]
            if step < steps - 1:
                result, leaving, payloads[micro] = leave(
                    step, micro, inflow, served[0], parts, arriving, later
                )
                inflows[micro] = next_section(leaving, 0)
            else:
                total = inflow.astype(jnp.float32) + served[0]
                for part in parts:
                    total = total + part.astype(jnp.float32)
                result = total.astype(jnp.bfloat16)
            results.append(result)
        outputs.append(jnp.stack(results))
    return jnp.stack(outputs)[:, None]


def solution(mesh):
    return jax.shard_map(
        local,
        mesh=mesh,
        in_specs=(
            P("section", None, "expert", None),
            P(None, None, "expert", None),
            P("section", None),
            P("section", "expert", None, None),
            P("section", "expert", None, None),
            P(None, "section", None, "expert", None),
            P(None, "section", None, "expert", None),
        ),
        out_specs=P(None, "section", None, "expert", None),
        check_vma=False,
    )
```

```python
import functools

import jax
import jax.numpy as jnp
from jax import lax
from jax.experimental import pallas as pl
from jax.experimental.pallas import tpu as pltpu
from jax.sharding import PartitionSpec as P

LANES = 128


def normalize(inflow, gain_row):
    widened = inflow.astype(jnp.float32)
    inverse_rms = lax.rsqrt(jnp.mean(widened * widened, axis=-1, keepdims=True) + 1e-06)
    return (widened * inverse_rms * gain_row).astype(jnp.bfloat16)


def token_weights(experts_all, width, ids, weights):
    steps, micro_count, top_count, tokens = ids.shape
    expert = lax.broadcasted_iota(jnp.int32, (experts_all, tokens), 0)
    columns = []
    for micro in range(micro_count):
        rows = []
        for step in range(steps):
            dense = jnp.zeros((experts_all, tokens), jnp.float32)
            for k in range(top_count):
                named = ids[step, micro, k : k + 1, :] == expert
                dense = dense + jnp.where(named, weights[step, micro, k : k + 1, :], 0.0)
            high = dense.astype(jnp.bfloat16).astype(jnp.float32)
            rows += [high, dense - high]
        empty = width - 2 * steps * experts_all
        if empty > 0:
            rows.append(jnp.zeros((empty, tokens), jnp.float32))
        columns.append(jnp.concatenate(rows, axis=0))
    return jnp.concatenate(columns, axis=1).T.astype(jnp.bfloat16).reshape(
        micro_count, tokens, width
    )


def first_kernel(experts_all, inflow_hbm, ids_hbm, weights_hbm, *refs):
    payloads, (inflow, ids, weights, sem) = refs[:-4], refs[-4:]
    copies = [
        pltpu.make_async_copy(source, target, sem.at[number])
        for number, (source, target) in enumerate(
            ((ids_hbm, ids), (weights_hbm, weights), (inflow_hbm, inflow))
        )
    ]
    for copy in copies:
        copy.start()
    for copy in copies:
        copy.wait()
    features = inflow.shape[-1]
    tails = token_weights(experts_all, payloads[0].shape[-1] - features, ids, weights)
    for micro, payload in enumerate(payloads):
        payload[:, :features] = inflow[micro]
        payload[:, features:] = tails[micro]


def first_payloads(inflow, ids, weights, experts_all):
    micro_count, tokens, features = inflow.shape
    width = -(-2 * experts_all * ids.shape[0] // LANES) * LANES
    return pl.pallas_call(
        functools.partial(first_kernel, experts_all),
        out_shape=(jax.ShapeDtypeStruct((tokens, features + width), jnp.bfloat16),) * micro_count,
        in_specs=[pl.BlockSpec(memory_space=pltpu.HBM)] * 3,
        out_specs=[pl.BlockSpec(memory_space=pltpu.VMEM)] * micro_count,
        scratch_shapes=[
            pltpu.VMEM(inflow.shape, inflow.dtype),
            pltpu.VMEM(ids.shape, ids.dtype),
            pltpu.VMEM(weights.shape, weights.dtype),
            pltpu.SemaphoreType.DMA((3,)),
        ],
        compiler_params=pltpu.CompilerParams(vmem_limit_bytes=60 * 1024 * 1024),
        name="first_payloads",
    )(inflow, ids, weights)


def hold_kernel(after, own_in, own_out, gain, kept):
    del after, own_in, own_out
    kept[...] = gain[...]


def hold(after, own_in, own_out, gain):
    whole = pl.BlockSpec(memory_space=pltpu.VMEM)
    return pl.pallas_call(
        hold_kernel,
        out_shape=jax.ShapeDtypeStruct(gain.shape, gain.dtype),
        in_specs=[pl.BlockSpec(memory_space=pl.ANY), whole, whole, whole],
        out_specs=whole,
        compiler_params=pltpu.CompilerParams(
            vmem_limit_bytes=2 * (own_in.size + own_out.size) + 8 * 1024 * 1024
        ),
        name="hold",
    )(after, own_in, own_out, gain)


def combine_kernel(near_sum, returned, own, *parts):
    own[...] = near_sum[0] + returned[0].astype(jnp.float32)
    for by, part in enumerate(parts, 1):
        part[...] = (near_sum[by] + returned[by].astype(jnp.float32)).astype(jnp.bfloat16)


def combine(near_sum, returned):
    blocks, tokens, features = near_sum.shape
    whole = pl.BlockSpec(memory_space=pltpu.VMEM)
    return pl.pallas_call(
        combine_kernel,
        out_shape=(jax.ShapeDtypeStruct((tokens, features), jnp.float32),)
        + (jax.ShapeDtypeStruct((tokens, features), jnp.bfloat16),) * (blocks - 1),
        in_specs=[whole] * 2,
        out_specs=[whole] * blocks,
        compiler_params=pltpu.CompilerParams(vmem_limit_bytes=8 * 1024 * 1024),
        name="combine",
    )(near_sum, returned)


def leave_kernel(step, micro, inflow, own, *refs):
    parts, (fresh, out, leaving) = refs[:-3], refs[-3:]
    total = inflow[...].reshape(own.shape).astype(jnp.float32) + own[...]
    for part in parts:
        total = total + part[...].astype(jnp.float32)
    result = total.astype(jnp.bfloat16)
    out[...] = result
    is_last = lax.axis_index("section") == lax.axis_size("section") - 1
    arrived = fresh[step, micro].astype(jnp.float32)
    leaving[...] = jnp.where(is_last, arrived, result.astype(jnp.float32)).astype(jnp.bfloat16)


def leave(step, micro, inflow, own, parts, fresh):
    whole = pl.BlockSpec(memory_space=pltpu.VMEM)
    return pl.pallas_call(
        functools.partial(leave_kernel, step, micro),
        out_shape=(jax.ShapeDtypeStruct(own.shape, jnp.bfloat16),) * 2,
        in_specs=[whole] * (3 + len(parts)),
        out_specs=[whole] * 2,
        compiler_params=pltpu.CompilerParams(vmem_limit_bytes=8 * 1024 * 1024),
        name="leave",
    )(inflow, own, *parts, fresh)


def swap_core(value):
    size = lax.axis_size("expert")
    return lax.ppermute(value, "expert", [(i, i ^ 1) for i in range(size)])


def swap_inner(value):
    size = lax.axis_size("expert")
    return lax.ppermute(value, "expert", [(i, i ^ 2) for i in range(size)])


def swap_outer(value, by):
    size = lax.axis_size("expert")
    return lax.ppermute(value, "expert", [(i, i ^ 4 * by) for i in range(size)])


def next_section(value, by):
    sections, size = lax.axis_size("section"), lax.axis_size("expert")
    pairs = [
        (s * size + i, (s + 1) % sections * size + (i ^ 4 * by))
        for s in range(sections)
        for i in range(size)
    ]
    return lax.ppermute(value, ("section", "expert"), pairs)


def previous_section(value):
    sections = lax.axis_size("section")
    return lax.ppermute(value, "section", [(s, (s - 1) % sections) for s in range(sections)])


def serve_kernel(
    features, hidden_count, chunk, experts_all, local_count, step,
    near, far, near_tail, far_tail, gain, own_in, far_in, own_out, far_out,
    near_sum, far_sum, rows, hidden,
):
    blocks, tokens = near.shape[:2]
    half = blocks * tokens
    for start, part in ((0, near), (half, far)):
        for block in range(blocks):
            at = start + block * tokens
            rows[at : at + tokens] = normalize(part[block, :, :features], gain[...])
    tail = jnp.concatenate(
        [part[:, :, features:].reshape(half, -1) for part in (near_tail, far_tail)]
    ).astype(jnp.float32)
    lane = lax.broadcasted_iota(jnp.int32, tail.shape, 1) - 2 * experts_all * step
    me = lax.axis_index("expert")
    total = None
    for side, (w_in, w_out) in enumerate(((own_in, own_out), (far_in, far_out))):
        for own in range(local_count):
            which = (me + side * (1 - 2 * (me % 2))) * local_count + own
            chosen = (lane == which) | (lane == which + experts_all)
            weight = jnp.sum(jnp.where(chosen, tail, 0.0), axis=-1, keepdims=True)
            for at in range(0, hidden_count, chunk):
                gate = jnp.dot(
                    rows[...], w_in[own, :, pl.ds(at, chunk)], preferred_element_type=jnp.float32
                )
                up = jnp.dot(
                    rows[...],
                    w_in[own, :, pl.ds(hidden_count + at, chunk)],
                    preferred_element_type=jnp.float32,
                )
                value = gate / (1.0 + jnp.exp(-gate)) * up * weight
                hidden[:, pl.ds(at, chunk)] = value.astype(jnp.bfloat16)
            out = jnp.dot(hidden[...], w_out[own], preferred_element_type=jnp.float32)
            total = out if total is None else total + out
    near_sum[...] = total[:half].reshape(near_sum.shape)
    far_sum[...] = total[half:].astype(jnp.bfloat16).reshape(far_sum.shape)


def serve(step, near, far, near_tail, far_tail, gain, own_in, far_in, own_out, far_out, experts_all):
    blocks, tokens, _ = near.shape
    local_count, features, _ = own_in.shape
    hidden_count = own_out.shape[1]
    chunk = 256 if hidden_count % 256 == 0 else hidden_count
    rows_all = 2 * blocks * tokens
    held = 2 * (own_in.size + own_out.size) * 2
    whole = pl.BlockSpec(memory_space=pltpu.VMEM)
    return pl.pallas_call(
        functools.partial(
            serve_kernel, features, hidden_count, chunk, experts_all, local_count, step
        ),
        out_shape=(
            jax.ShapeDtypeStruct((blocks, tokens, features), jnp.float32),
            jax.ShapeDtypeStruct((blocks, tokens, features), jnp.bfloat16),
        ),
        in_specs=[whole] * 9,
        out_specs=[whole] * 2,
        scratch_shapes=[
            pltpu.VMEM((rows_all, features), jnp.bfloat16),
            pltpu.VMEM((rows_all, hidden_count), jnp.bfloat16),
        ],
        compiler_params=pltpu.CompilerParams(vmem_limit_bytes=held + 10 * 1024 * 1024),
        cost_estimate=pl.CostEstimate(
            flops=2 * rows_all * 2 * local_count * 3 * features * hidden_count,
            bytes_accessed=held,
            transcendentals=rows_all * 2 * local_count * hidden_count,
        ),
        name="serve",
    )(near, far, near_tail, far_tail, gain, own_in, far_in, own_out, far_out)


def tied(*values):
    return lax.optimization_barrier(values)


def local(in_flight, arriving, norm_gain, gate_up, w_down, expert_ids, route_weights):
    owners = lax.axis_size("expert")
    outer = owners // 4
    local_count = gate_up.shape[1]
    experts_all = owners * local_count
    steps = expert_ids.shape[0]
    micro_count = in_flight.shape[1]
    micros = range(micro_count)
    payloads = first_payloads(
        in_flight[0],
        jnp.swapaxes(expert_ids[:, 0], -1, -2),
        jnp.swapaxes(route_weights[:, 0], -1, -2),
        experts_all,
    )
    *payloads, gate_up, w_down = tied(*payloads, gate_up, w_down)
    own_in, own_out = gate_up[0], w_down[0]
    far_in, far_out = swap_core(own_in), swap_core(own_out)
    gain = norm_gain
    inflows = [in_flight[0, micro] for micro in micros]
    outputs = []
    for step in range(steps):
        near, far, own, parts, results = [], [], [], [], []
        for micro in micros:
            payload = payloads[micro]
            if step == 0:
                blocks = [swap_outer(payload, by) for by in range(outer - 1, 0, -1)] + [payload]
            else:
                blocks = [next_section(payload, by) for by in range(outer - 1, -1, -1)]
                inflows[micro] = blocks[-1]
            near.append(jnp.stack(blocks[::-1]))
            if step == 0 and micro == 0:
                gain = hold(near[0], own_in, own_out, gain)
            far.append(swap_inner(near[micro]))
        if step == 0:
            near_tail, far_tail = near, far
        returned = []
        for micro in micros:
            near_sum, far_sum = serve(
                step, near[micro], far[micro], near_tail[micro], far_tail[micro], gain,
                own_in, far_in, own_out, far_out, experts_all,
            )
            own.append(near_sum)
            returned.append(swap_inner(far_sum))
        for micro in micros:
            own[micro], *blocks = combine(own[micro], returned[micro])
            parts.append([swap_outer(blocks[by - 1], by) for by in range(outer - 1, 0, -1)])
        for micro in micros:
            if step < steps - 1:
                if micro < micro_count - 1:
                    parts[micro][0], own[micro + 1] = tied(parts[micro][0], own[micro + 1])
                result, payloads[micro] = leave(
                    step, micro, inflows[micro], own[micro], parts[micro], arriving
                )
            else:
                total = inflows[micro].astype(jnp.float32) + own[micro]
                for part in parts[micro]:
                    total = total + part.astype(jnp.float32)
                result = total.astype(jnp.bfloat16)
            results.append(result)
        outputs.append(jnp.stack(results))
    return jnp.stack(outputs)[:, None]


def solution(mesh):
    return jax.shard_map(
        local,
        mesh=mesh,
        in_specs=(
            P("section", None, "expert", None),
            P(None, None, "expert", None),
            P("section", None),
            P("section", "expert", None, None),
            P("section", "expert", None, None),
            P(None, "section", None, "expert", None),
            P(None, "section", None, "expert", None),
        ),
        out_specs=P(None, "section", None, "expert", None),
        check_vma=False,
    )
```

```python
import functools

import jax
import jax.numpy as jnp
from jax import lax
from jax.experimental import pallas as pl
from jax.experimental.pallas import tpu as pltpu
from jax.sharding import PartitionSpec as P

LANES = 128


def normalize(inflow, gain_row):
    widened = inflow.astype(jnp.float32)
    inverse_rms = lax.rsqrt(jnp.mean(widened * widened, axis=-1, keepdims=True) + 1e-06)
    return (widened * inverse_rms * gain_row).astype(jnp.bfloat16)


def token_weights(experts_all, width, ids, weights):
    steps, micro_count, top_count, tokens = ids.shape
    expert = lax.broadcasted_iota(jnp.int32, (experts_all, tokens), 0)
    columns = []
    for micro in range(micro_count):
        rows = []
        for step in range(steps):
            dense = jnp.zeros((experts_all, tokens), jnp.float32)
            for k in range(top_count):
                named = ids[step, micro, k : k + 1, :] == expert
                dense = dense + jnp.where(named, weights[step, micro, k : k + 1, :], 0.0)
            high = dense.astype(jnp.bfloat16).astype(jnp.float32)
            rows += [high, dense - high]
        empty = width - 2 * steps * experts_all
        if empty > 0:
            rows.append(jnp.zeros((empty, tokens), jnp.float32))
        columns.append(jnp.concatenate(rows, axis=0))
    return jnp.concatenate(columns, axis=1).T.astype(jnp.bfloat16).reshape(
        micro_count, tokens, width
    )


def first_kernel(experts_all, inflow_hbm, ids_hbm, weights_hbm, *refs):
    payloads, (inflow, ids, weights, sem) = refs[:-4], refs[-4:]
    copies = [
        pltpu.make_async_copy(source, target, sem.at[number])
        for number, (source, target) in enumerate(
            ((ids_hbm, ids), (weights_hbm, weights), (inflow_hbm, inflow))
        )
    ]
    for copy in copies:
        copy.start()
    for copy in copies:
        copy.wait()
    features = inflow.shape[-1]
    tails = token_weights(experts_all, payloads[0].shape[-1] - features, ids, weights)
    for micro, payload in enumerate(payloads):
        payload[:, :features] = inflow[micro]
        payload[:, features:] = tails[micro]


def first_payloads(inflow, ids, weights, experts_all):
    micro_count, tokens, features = inflow.shape
    width = -(-2 * experts_all * ids.shape[0] // LANES) * LANES
    return pl.pallas_call(
        functools.partial(first_kernel, experts_all),
        out_shape=(jax.ShapeDtypeStruct((tokens, features + width), jnp.bfloat16),) * micro_count,
        in_specs=[pl.BlockSpec(memory_space=pltpu.HBM)] * 3,
        out_specs=[pl.BlockSpec(memory_space=pltpu.VMEM)] * micro_count,
        scratch_shapes=[
            pltpu.VMEM(inflow.shape, inflow.dtype),
            pltpu.VMEM(ids.shape, ids.dtype),
            pltpu.VMEM(weights.shape, weights.dtype),
            pltpu.SemaphoreType.DMA((3,)),
        ],
        compiler_params=pltpu.CompilerParams(vmem_limit_bytes=60 * 1024 * 1024),
        name="first_payloads",
    )(inflow, ids, weights)


def hold_kernel(after, own_in, own_out, gain, kept):
    del after, own_in, own_out
    kept[...] = gain[...]


def hold(after, own_in, own_out, gain):
    whole = pl.BlockSpec(memory_space=pltpu.VMEM)
    return pl.pallas_call(
        hold_kernel,
        out_shape=jax.ShapeDtypeStruct(gain.shape, gain.dtype),
        in_specs=[pl.BlockSpec(memory_space=pl.ANY), whole, whole, whole],
        out_specs=whole,
        compiler_params=pltpu.CompilerParams(
            vmem_limit_bytes=2 * (own_in.size + own_out.size) + 8 * 1024 * 1024
        ),
        name="hold",
    )(after, own_in, own_out, gain)


def combine_kernel(near_sum, returned, own, *parts):
    own[...] = near_sum[0] + returned[0].astype(jnp.float32)
    for by, part in enumerate(parts, 1):
        part[...] = (near_sum[by] + returned[by].astype(jnp.float32)).astype(jnp.bfloat16)


def combine(near_sum, returned):
    blocks, tokens, features = near_sum.shape
    whole = pl.BlockSpec(memory_space=pltpu.VMEM)
    return pl.pallas_call(
        combine_kernel,
        out_shape=(jax.ShapeDtypeStruct((tokens, features), jnp.float32),)
        + (jax.ShapeDtypeStruct((tokens, features), jnp.bfloat16),) * (blocks - 1),
        in_specs=[whole] * 2,
        out_specs=[whole] * blocks,
        compiler_params=pltpu.CompilerParams(vmem_limit_bytes=8 * 1024 * 1024),
        name="combine",
    )(near_sum, returned)


def leave_kernel(step, micro_count, *refs):
    fresh, leaving = refs[-2 - micro_count], refs[-1]
    results = refs[-1 - micro_count : -1]
    each = (len(refs) - 2 - micro_count) // micro_count
    is_last = lax.axis_index("section") == lax.axis_size("section") - 1
    for micro, out in enumerate(results):
        inflow, own, *parts = refs[micro * each : (micro + 1) * each]
        total = inflow[...].astype(jnp.float32) + own[...]
        for part in parts:
            total = total + part[...].astype(jnp.float32)
        result = total.astype(jnp.bfloat16)
        out[...] = result
        arrived = fresh[step, micro].astype(jnp.float32)
        gone = jnp.where(is_last, arrived, result.astype(jnp.float32))
        leaving[micro] = gone.astype(jnp.bfloat16)


def leave(step, inflows, own, parts, fresh):
    micro_count = len(own)
    rows = jax.ShapeDtypeStruct(own[0].shape, jnp.bfloat16)
    operands = []
    for micro in range(micro_count):
        operands += [inflows[micro], own[micro], *parts[micro]]
    operands.append(fresh)
    whole = pl.BlockSpec(memory_space=pltpu.VMEM)
    return pl.pallas_call(
        functools.partial(leave_kernel, step, micro_count),
        out_shape=(rows,) * micro_count
        + (jax.ShapeDtypeStruct((micro_count,) + rows.shape, rows.dtype),),
        in_specs=[whole] * len(operands),
        out_specs=[whole] * (micro_count + 1),
        compiler_params=pltpu.CompilerParams(vmem_limit_bytes=8 * 1024 * 1024),
        name="leave",
    )(*operands)


def swap_core(value):
    size = lax.axis_size("expert")
    return lax.ppermute(value, "expert", [(i, i ^ 1) for i in range(size)])


def swap_inner(value):
    size = lax.axis_size("expert")
    return lax.ppermute(value, "expert", [(i, i ^ 2) for i in range(size)])


def swap_outer(value, by):
    size = lax.axis_size("expert")
    return lax.ppermute(value, "expert", [(i, i ^ 4 * by) for i in range(size)])


def next_section(value, by):
    sections, size = lax.axis_size("section"), lax.axis_size("expert")
    pairs = [
        (s * size + i, (s + 1) % sections * size + (i ^ 4 * by))
        for s in range(sections)
        for i in range(size)
    ]
    return lax.ppermute(value, ("section", "expert"), pairs)


def previous_section(value):
    sections = lax.axis_size("section")
    return lax.ppermute(value, "section", [(s, (s - 1) % sections) for s in range(sections)])


def serve_kernel(
    features, hidden_count, chunk, experts_all, local_count, step,
    near, far, near_tail, far_tail, gain, own_in, far_in, own_out, far_out,
    near_sum, far_sum, rows, hidden,
):
    blocks, tokens = near.shape[:2]
    half = blocks * tokens
    for start, part in ((0, near), (half, far)):
        for block in range(blocks):
            at = start + block * tokens
            rows[at : at + tokens] = normalize(part[block, :, :features], gain[...])
    tail = jnp.concatenate(
        [part[:, :, features:].reshape(half, -1) for part in (near_tail, far_tail)]
    ).astype(jnp.float32)
    lane = lax.broadcasted_iota(jnp.int32, tail.shape, 1) - 2 * experts_all * step
    me = lax.axis_index("expert")
    total = None
    for side, (w_in, w_out) in enumerate(((own_in, own_out), (far_in, far_out))):
        for own in range(local_count):
            which = (me + side * (1 - 2 * (me % 2))) * local_count + own
            chosen = (lane == which) | (lane == which + experts_all)
            weight = jnp.sum(jnp.where(chosen, tail, 0.0), axis=-1, keepdims=True)
            for at in range(0, hidden_count, chunk):
                gate = jnp.dot(
                    rows[...], w_in[own, :, pl.ds(at, chunk)], preferred_element_type=jnp.float32
                )
                up = jnp.dot(
                    rows[...],
                    w_in[own, :, pl.ds(hidden_count + at, chunk)],
                    preferred_element_type=jnp.float32,
                )
                value = gate / (1.0 + jnp.exp(-gate)) * up * weight
                hidden[:, pl.ds(at, chunk)] = value.astype(jnp.bfloat16)
            out = jnp.dot(hidden[...], w_out[own], preferred_element_type=jnp.float32)
            total = out if total is None else total + out
    near_sum[...] = total[:half].reshape(near_sum.shape)
    far_sum[...] = total[half:].astype(jnp.bfloat16).reshape(far_sum.shape)


def serve(step, near, far, near_tail, far_tail, gain, own_in, far_in, own_out, far_out, experts_all):
    blocks, tokens, _ = near.shape
    local_count, features, _ = own_in.shape
    hidden_count = own_out.shape[1]
    chunk = 256 if hidden_count % 256 == 0 else hidden_count
    rows_all = 2 * blocks * tokens
    held = 2 * (own_in.size + own_out.size) * 2
    whole = pl.BlockSpec(memory_space=pltpu.VMEM)
    return pl.pallas_call(
        functools.partial(
            serve_kernel, features, hidden_count, chunk, experts_all, local_count, step
        ),
        out_shape=(
            jax.ShapeDtypeStruct((blocks, tokens, features), jnp.float32),
            jax.ShapeDtypeStruct((blocks, tokens, features), jnp.bfloat16),
        ),
        in_specs=[whole] * 9,
        out_specs=[whole] * 2,
        scratch_shapes=[
            pltpu.VMEM((rows_all, features), jnp.bfloat16),
            pltpu.VMEM((rows_all, hidden_count), jnp.bfloat16),
        ],
        compiler_params=pltpu.CompilerParams(vmem_limit_bytes=held + 10 * 1024 * 1024),
        cost_estimate=pl.CostEstimate(
            flops=2 * rows_all * 2 * local_count * 3 * features * hidden_count,
            bytes_accessed=held,
            transcendentals=rows_all * 2 * local_count * hidden_count,
        ),
        name="serve",
    )(near, far, near_tail, far_tail, gain, own_in, far_in, own_out, far_out)


def tied(*values):
    return lax.optimization_barrier(values)


def local(in_flight, arriving, norm_gain, gate_up, w_down, expert_ids, route_weights):
    owners = lax.axis_size("expert")
    outer = owners // 4
    local_count = gate_up.shape[1]
    experts_all = owners * local_count
    steps = expert_ids.shape[0]
    micro_count = in_flight.shape[1]
    micros = range(micro_count)
    payloads = first_payloads(
        in_flight[0],
        jnp.swapaxes(expert_ids[:, 0], -1, -2),
        jnp.swapaxes(route_weights[:, 0], -1, -2),
        experts_all,
    )
    *payloads, gate_up, w_down = tied(*payloads, gate_up, w_down)
    own_in, own_out = gate_up[0], w_down[0]
    far_in, far_out = swap_core(own_in), swap_core(own_out)
    gain = norm_gain
    inflows = [in_flight[0, micro] for micro in micros]
    outputs = []
    for step in range(steps):
        near, far, own, parts, results = [], [], [], [], []
        if step > 0:
            hopped = [next_section(leaving, by) for by in range(outer - 1, -1, -1)]
        for micro in micros:
            if step == 0:
                payload = payloads[micro]
                blocks = [swap_outer(payload, by) for by in range(outer - 1, 0, -1)] + [payload]
            else:
                blocks = [block[micro] for block in hopped]
                inflows[micro] = blocks[-1]
            near.append(jnp.stack(blocks[::-1]))
            if step == 0 and micro == 0:
                gain = hold(payload, own_in, own_out, gain)
                near[0], gain = tied(near[0], gain)
            far.append(swap_inner(near[micro]))
        if step == 0:
            near_tail, far_tail = near, far
        returned = []
        for micro in micros:
            near_sum, far_sum = serve(
                step, near[micro], far[micro], near_tail[micro], far_tail[micro], gain,
                own_in, far_in, own_out, far_out, experts_all,
            )
            own.append(near_sum)
            returned.append(swap_inner(far_sum))
        for micro in micros:
            own[micro], *blocks = combine(own[micro], returned[micro])
            parts.append([swap_outer(blocks[by - 1], by) for by in range(outer - 1, 0, -1)])
        if step < steps - 1:
            *results, leaving = leave(step, inflows, own, parts, arriving)
        else:
            for micro in micros:
                total = inflows[micro].astype(jnp.float32) + own[micro]
                for part in parts[micro]:
                    total = total + part.astype(jnp.float32)
                results.append(total.astype(jnp.bfloat16))
        outputs.append(jnp.stack(results))
    return jnp.stack(outputs)[:, None]


def solution(mesh):
    return jax.shard_map(
        local,
        mesh=mesh,
        in_specs=(
            P("section", None, "expert", None),
            P(None, None, "expert", None),
            P("section", None),
            P("section", "expert", None, None),
            P("section", "expert", None, None),
            P(None, "section", None, "expert", None),
            P(None, "section", None, "expert", None),
        ),
        out_specs=P(None, "section", None, "expert", None),
        check_vma=False,
    )
```

```python
import functools

import jax
import jax.numpy as jnp
from jax import lax
from jax.experimental import pallas as pl
from jax.experimental.pallas import tpu as pltpu
from jax.sharding import PartitionSpec as P

LANES = 128


def normalize(inflow, gain_row):
    widened = inflow.astype(jnp.float32)
    inverse_rms = lax.rsqrt(jnp.mean(widened * widened, axis=-1, keepdims=True) + 1e-06)
    return (widened * inverse_rms * gain_row).astype(jnp.bfloat16)


def token_weights(experts_all, width, ids, weights):
    steps, micro_count, top_count, tokens = ids.shape
    expert = lax.broadcasted_iota(jnp.int32, (experts_all, tokens), 0)
    columns = []
    for micro in range(micro_count):
        rows = []
        for step in range(steps):
            dense = jnp.zeros((experts_all, tokens), jnp.float32)
            for k in range(top_count):
                named = ids[step, micro, k : k + 1, :] == expert
                dense = dense + jnp.where(named, weights[step, micro, k : k + 1, :], 0.0)
            high = dense.astype(jnp.bfloat16).astype(jnp.float32)
            rows += [high, dense - high]
        empty = width - 2 * steps * experts_all
        if empty > 0:
            rows.append(jnp.zeros((empty, tokens), jnp.float32))
        columns.append(jnp.concatenate(rows, axis=0))
    return jnp.concatenate(columns, axis=1).T.astype(jnp.bfloat16).reshape(
        micro_count, tokens, width
    )


def first_kernel(experts_all, inflow_hbm, ids_hbm, weights_hbm, *refs):
    both, first, inflow, ids, weights, sem = refs
    copies = [
        pltpu.make_async_copy(source, target, sem.at[number])
        for number, (source, target) in enumerate(
            ((ids_hbm, ids), (weights_hbm, weights), (inflow_hbm, inflow))
        )
    ]
    for copy in copies:
        copy.start()
    for copy in copies:
        copy.wait()
    features = inflow.shape[-1]
    tails = token_weights(experts_all, both.shape[-1] - features, ids, weights)
    both[:, :, :features] = inflow[...]
    both[:, :, features:] = tails
    first[:, :features] = inflow[0]
    first[:, features:] = tails[0]


def first_payloads(inflow, ids, weights, experts_all):
    micro_count, tokens, features = inflow.shape
    width = -(-2 * experts_all * ids.shape[0] // LANES) * LANES
    return pl.pallas_call(
        functools.partial(first_kernel, experts_all),
        out_shape=(
            jax.ShapeDtypeStruct((micro_count, tokens, features + width), jnp.bfloat16),
            jax.ShapeDtypeStruct((tokens, features + width), jnp.bfloat16),
        ),
        in_specs=[pl.BlockSpec(memory_space=pltpu.HBM)] * 3,
        out_specs=[pl.BlockSpec(memory_space=pltpu.VMEM)] * 2,
        scratch_shapes=[
            pltpu.VMEM(inflow.shape, inflow.dtype),
            pltpu.VMEM(ids.shape, ids.dtype),
            pltpu.VMEM(weights.shape, weights.dtype),
            pltpu.SemaphoreType.DMA((3,)),
        ],
        compiler_params=pltpu.CompilerParams(vmem_limit_bytes=60 * 1024 * 1024),
        name="first_payloads",
    )(inflow, ids, weights)


def hold_kernel(after, own_in, own_out, gain, kept):
    del after, own_in, own_out
    kept[...] = gain[...]


def hold(after, own_in, own_out, gain):
    whole = pl.BlockSpec(memory_space=pltpu.VMEM)
    return pl.pallas_call(
        hold_kernel,
        out_shape=jax.ShapeDtypeStruct(gain.shape, gain.dtype),
        in_specs=[pl.BlockSpec(memory_space=pl.ANY), whole, whole, whole],
        out_specs=whole,
        compiler_params=pltpu.CompilerParams(
            vmem_limit_bytes=2 * (own_in.size + own_out.size) + 8 * 1024 * 1024
        ),
        name="hold",
    )(after, own_in, own_out, gain)


def combine_kernel(near_sum, returned, own, *parts):
    own[...] = near_sum[0] + returned[0].astype(jnp.float32)
    for by, part in enumerate(parts, 1):
        part[...] = (near_sum[by] + returned[by].astype(jnp.float32)).astype(jnp.bfloat16)


def combine(near_sum, returned):
    blocks, tokens, features = near_sum.shape
    whole = pl.BlockSpec(memory_space=pltpu.VMEM)
    return pl.pallas_call(
        combine_kernel,
        out_shape=(jax.ShapeDtypeStruct((tokens, features), jnp.float32),)
        + (jax.ShapeDtypeStruct((tokens, features), jnp.bfloat16),) * (blocks - 1),
        in_specs=[whole] * 2,
        out_specs=[whole] * blocks,
        compiler_params=pltpu.CompilerParams(vmem_limit_bytes=8 * 1024 * 1024),
        name="combine",
    )(near_sum, returned)


def halve_kernel(kept, received, own, out):
    half = own.shape[0]
    own[...] = kept[:half] + received[:half].astype(jnp.float32)
    out[...] = (kept[half:] + received[half:].astype(jnp.float32)).astype(jnp.bfloat16)


def halve(kept, received):
    blocks, tokens, features = kept.shape
    whole = pl.BlockSpec(memory_space=pltpu.VMEM)
    return pl.pallas_call(
        halve_kernel,
        out_shape=(
            jax.ShapeDtypeStruct((blocks // 2, tokens, features), jnp.float32),
            jax.ShapeDtypeStruct((blocks // 2, tokens, features), jnp.bfloat16),
        ),
        in_specs=[whole] * 2,
        out_specs=[whole] * 2,
        compiler_params=pltpu.CompilerParams(vmem_limit_bytes=8 * 1024 * 1024),
        name="halve",
    )(kept, received)


def leave_kernel(step, counts, *refs):
    outs = len(counts) + 2
    fresh, results, both, first = refs[-outs - 1], refs[-outs:-2], refs[-2], refs[-1]
    is_last = lax.axis_index("section") == lax.axis_size("section") - 1
    at = 0
    for micro, out in enumerate(results):
        inflow, *parts = refs[at : at + counts[micro]]
        at += counts[micro]
        total = inflow[...].astype(jnp.float32)
        for part in parts:
            total = total + part[...].reshape(out.shape).astype(jnp.float32)
        result = total.astype(jnp.bfloat16)
        out[...] = result
        arrived = fresh[step, micro].astype(jnp.float32)
        gone = jnp.where(is_last, arrived, result.astype(jnp.float32)).astype(jnp.bfloat16)
        both[micro] = gone
        if micro == 0:
            first[...] = gone


def leave(step, inflows, parts, fresh):
    rows = jax.ShapeDtypeStruct(inflows[0].shape, jnp.bfloat16)
    operands, counts = [], []
    for inflow, some in zip(inflows, parts):
        operands += [inflow, *some]
        counts.append(1 + len(some))
    operands.append(fresh)
    whole = pl.BlockSpec(memory_space=pltpu.VMEM)
    return pl.pallas_call(
        functools.partial(leave_kernel, step, counts),
        out_shape=(rows,) * len(inflows)
        + (jax.ShapeDtypeStruct((len(inflows),) + rows.shape, rows.dtype), rows),
        in_specs=[whole] * len(operands),
        out_specs=[whole] * (len(inflows) + 2),
        compiler_params=pltpu.CompilerParams(vmem_limit_bytes=8 * 1024 * 1024),
        name="leave",
    )(*operands)


def swapped(value, mask):
    size = lax.axis_size("expert")
    return lax.ppermute(value, "expert", [(i, i ^ mask) for i in range(size)])


def next_section(value, by):
    sections, size = lax.axis_size("section"), lax.axis_size("expert")
    pairs = [
        (s * size + i, (s + 1) % sections * size + (i ^ 4 * by))
        for s in range(sections)
        for i in range(size)
    ]
    return lax.ppermute(value, ("section", "expert"), pairs)


def previous_section(value):
    sections = lax.axis_size("section")
    return lax.ppermute(value, "section", [(s, (s - 1) % sections) for s in range(sections)])


def serve_kernel(
    features, hidden_count, chunk, experts_all, local_count, step,
    near, far, near_tail, far_tail, gain, own_in, far_in, own_out, far_out,
    near_sum, far_sum, rows, hidden,
):
    blocks, tokens = near.shape[:2]
    half = blocks * tokens
    for start, part in ((0, near), (half, far)):
        for block in range(blocks):
            at = start + block * tokens
            rows[at : at + tokens] = normalize(part[block, :, :features], gain[...])
    tail = jnp.concatenate(
        [part[:, :, features:].reshape(half, -1) for part in (near_tail, far_tail)]
    ).astype(jnp.float32)
    lane = lax.broadcasted_iota(jnp.int32, tail.shape, 1) - 2 * experts_all * step
    me = lax.axis_index("expert")
    total = None
    for side, (w_in, w_out) in enumerate(((own_in, own_out), (far_in, far_out))):
        for own in range(local_count):
            which = (me + side * (1 - 2 * (me % 2))) * local_count + own
            chosen = (lane == which) | (lane == which + experts_all)
            weight = jnp.sum(jnp.where(chosen, tail, 0.0), axis=-1, keepdims=True)
            for at in range(0, hidden_count, chunk):
                gate = jnp.dot(
                    rows[...], w_in[own, :, pl.ds(at, chunk)], preferred_element_type=jnp.float32
                )
                up = jnp.dot(
                    rows[...],
                    w_in[own, :, pl.ds(hidden_count + at, chunk)],
                    preferred_element_type=jnp.float32,
                )
                value = gate / (1.0 + jnp.exp(-gate)) * up * weight
                hidden[:, pl.ds(at, chunk)] = value.astype(jnp.bfloat16)
            out = jnp.dot(hidden[...], w_out[own], preferred_element_type=jnp.float32)
            total = out if total is None else total + out
    near_sum[...] = total[:half].reshape(near_sum.shape)
    far_sum[...] = total[half:].astype(jnp.bfloat16).reshape(far_sum.shape)


def serve(step, near, far, near_tail, far_tail, gain, own_in, far_in, own_out, far_out, experts_all):
    blocks, tokens, _ = near.shape
    local_count, features, _ = own_in.shape
    hidden_count = own_out.shape[1]
    chunk = 256 if hidden_count % 256 == 0 else hidden_count
    rows_all = 2 * blocks * tokens
    held = 2 * (own_in.size + own_out.size) * 2
    whole = pl.BlockSpec(memory_space=pltpu.VMEM)
    return pl.pallas_call(
        functools.partial(
            serve_kernel, features, hidden_count, chunk, experts_all, local_count, step
        ),
        out_shape=(
            jax.ShapeDtypeStruct((blocks, tokens, features), jnp.float32),
            jax.ShapeDtypeStruct((blocks, tokens, features), jnp.bfloat16),
        ),
        in_specs=[whole] * 9,
        out_specs=[whole] * 2,
        scratch_shapes=[
            pltpu.VMEM((rows_all, features), jnp.bfloat16),
            pltpu.VMEM((rows_all, hidden_count), jnp.bfloat16),
        ],
        compiler_params=pltpu.CompilerParams(vmem_limit_bytes=held + 10 * 1024 * 1024),
        cost_estimate=pl.CostEstimate(
            flops=2 * rows_all * 2 * local_count * 3 * features * hidden_count,
            bytes_accessed=held,
            transcendentals=rows_all * 2 * local_count * hidden_count,
        ),
        name="serve",
    )(near, far, near_tail, far_tail, gain, own_in, far_in, own_out, far_out)


def tied(*values):
    return lax.optimization_barrier(values)


def local(in_flight, arriving, norm_gain, gate_up, w_down, expert_ids, route_weights):
    owners = lax.axis_size("expert")
    outer = owners // 4
    local_count = gate_up.shape[1]
    experts_all = owners * local_count
    steps = expert_ids.shape[0]
    micro_count = in_flight.shape[1]
    micros = range(micro_count)
    both, first = first_payloads(
        in_flight[0],
        jnp.swapaxes(expert_ids[:, 0], -1, -2),
        jnp.swapaxes(route_weights[:, 0], -1, -2),
        experts_all,
    )
    both, first, gate_up, w_down = tied(both, first, gate_up, w_down)
    own_in, own_out = gate_up[0], w_down[0]
    far_in, far_out = swapped(own_in, 1), swapped(own_out, 1)
    gain = hold(first, own_in, own_out, norm_gain)
    inflows = [in_flight[0, micro] for micro in micros]
    top = outer // 2
    masks = [4 * bit for bit in (1 << place for place in range(outer.bit_length())) if bit < outer]
    masks = masks[-2:0:-1] + [2] + masks[:1] * (len(masks) > 1)
    tails = [None] * micro_count
    outputs = []
    for step in range(steps):
        if step == 0:
            here = both
            there = swapped(both, 4 * top)
            blocks = {by: swapped(first, 4 * by) for by in range(outer - 1, 0, -1) if by != top}
        else:
            there = next_section(both, top)
            blocks = {by: next_section(first, by) for by in range(outer - 1, 0, -1) if by != top}
            here = next_section(both, 0)
            inflows = [here[micro] for micro in micros]
        near, far = [], []
        here, there, *others = tied(here, there, *blocks.values())
        blocks = dict(zip(blocks, others))
        if step == 0:
            there, gain = tied(there, gain)
        for micro in micros:
            if micro == 0:
                blocks[0], blocks[top] = here[0], there[0]
                value = jnp.stack([blocks[by] for by in range(outer)])
                last = 2
            else:
                value = jnp.stack([here[micro], there[micro]])
                for mask in masks[:-1]:
                    value = jnp.concatenate([value, swapped(value, mask)])
                last = masks[-1]
            near.append(value)
            far.append(swapped(value, last))
        if step == 0:
            tails = list(zip(near, far))
        sums, sent = [], []
        for micro in micros:
            if micro > 0:
                far[micro], sums[micro - 1] = tied(far[micro], sums[micro - 1])
            one_sum, one_sent = serve(
                step, near[micro], far[micro], *tails[micro], gain,
                own_in, far_in, own_out, far_out, experts_all,
            )
            sums.append(one_sum)
            sent.append(one_sent)
        parts = []
        for micro in micros:
            if micro == 0:
                own, *sends = combine(sums[0], swapped(sent[0], 2))
                returned = [swapped(sends[by - 1], 4 * by) for by in range(outer - 1, 0, -1)]
            else:
                own, received = sums[micro], swapped(sent[micro], masks[-1])
                for mask in ([4 * top] + masks[:-1])[::-1]:
                    own, rest = halve(own, received)
                    received = swapped(rest, mask)
                returned = [received]
            parts.append([own, *returned])
        if step < steps - 1:
            *results, both, first = leave(step, inflows, parts, arriving)
        else:
            results = []
            for micro in micros:
                total = inflows[micro].astype(jnp.float32)
                for part in parts[micro]:
                    total = total + part.reshape(total.shape).astype(jnp.float32)
                results.append(total.astype(jnp.bfloat16))
        outputs.append(jnp.stack(results))
    return jnp.stack(outputs)[:, None]


def solution(mesh):
    return jax.shard_map(
        local,
        mesh=mesh,
        in_specs=(
            P("section", None, "expert", None),
            P(None, None, "expert", None),
            P("section", None),
            P("section", "expert", None, None),
            P("section", "expert", None, None),
            P(None, "section", None, "expert", None),
            P(None, "section", None, "expert", None),
        ),
        out_specs=P(None, "section", None, "expert", None),
        check_vma=False,
    )
```

```python
import functools

import jax
import jax.numpy as jnp
from jax import lax
from jax.experimental import pallas as pl
from jax.experimental.pallas import tpu as pltpu
from jax.sharding import PartitionSpec as P

LANES = 128


def normalize(inflow, gain_row):
    widened = inflow.astype(jnp.float32)
    inverse_rms = lax.rsqrt(jnp.mean(widened * widened, axis=-1, keepdims=True) + 1e-06)
    return (widened * inverse_rms * gain_row).astype(jnp.bfloat16)


def token_weights(experts_all, width, ids, weights):
    steps, micro_count, top_count, tokens = ids.shape
    expert = lax.broadcasted_iota(jnp.int32, (experts_all, tokens), 0)
    columns = []
    for micro in range(micro_count):
        rows = []
        for step in range(steps):
            dense = jnp.zeros((experts_all, tokens), jnp.float32)
            for k in range(top_count):
                named = ids[step, micro, k : k + 1, :] == expert
                dense = dense + jnp.where(named, weights[step, micro, k : k + 1, :], 0.0)
            high = dense.astype(jnp.bfloat16).astype(jnp.float32)
            rows += [high, dense - high]
        empty = width - 2 * steps * experts_all
        if empty > 0:
            rows.append(jnp.zeros((empty, tokens), jnp.float32))
        columns.append(jnp.concatenate(rows, axis=0))
    return jnp.concatenate(columns, axis=1).T.astype(jnp.bfloat16).reshape(
        micro_count, tokens, width
    )


def first_kernel(experts_all, inflow_hbm, ids_hbm, weights_hbm, *refs):
    both, first, inflow, ids, weights, sem = refs
    copies = [
        pltpu.make_async_copy(source, target, sem.at[number])
        for number, (source, target) in enumerate(
            ((ids_hbm, ids), (weights_hbm, weights), (inflow_hbm, inflow))
        )
    ]
    for copy in copies:
        copy.start()
    for copy in copies:
        copy.wait()
    features = inflow.shape[-1]
    tails = token_weights(experts_all, both.shape[-1] - features, ids, weights)
    both[:, :, :features] = inflow[...]
    both[:, :, features:] = tails
    first[:, :features] = inflow[0]
    first[:, features:] = tails[0]


def first_payloads(inflow, ids, weights, experts_all):
    micro_count, tokens, features = inflow.shape
    width = -(-2 * experts_all * ids.shape[0] // LANES) * LANES
    return pl.pallas_call(
        functools.partial(first_kernel, experts_all),
        out_shape=(
            jax.ShapeDtypeStruct((micro_count, tokens, features + width), jnp.bfloat16),
            jax.ShapeDtypeStruct((tokens, features + width), jnp.bfloat16),
        ),
        in_specs=[pl.BlockSpec(memory_space=pltpu.HBM)] * 3,
        out_specs=[pl.BlockSpec(memory_space=pltpu.VMEM)] * 2,
        scratch_shapes=[
            pltpu.VMEM(inflow.shape, inflow.dtype),
            pltpu.VMEM(ids.shape, ids.dtype),
            pltpu.VMEM(weights.shape, weights.dtype),
            pltpu.SemaphoreType.DMA((3,)),
        ],
        compiler_params=pltpu.CompilerParams(vmem_limit_bytes=60 * 1024 * 1024),
        name="first_payloads",
    )(inflow, ids, weights)


def hold_kernel(after, own_in, own_out, gain, kept):
    del after, own_in, own_out
    kept[...] = gain[...]


def hold(after, own_in, own_out, gain):
    whole = pl.BlockSpec(memory_space=pltpu.VMEM)
    return pl.pallas_call(
        hold_kernel,
        out_shape=jax.ShapeDtypeStruct(gain.shape, gain.dtype),
        in_specs=[pl.BlockSpec(memory_space=pl.ANY), whole, whole, whole],
        out_specs=whole,
        compiler_params=pltpu.CompilerParams(
            vmem_limit_bytes=2 * (own_in.size + own_out.size) + 8 * 1024 * 1024
        ),
        name="hold",
    )(after, own_in, own_out, gain)


def combine_kernel(near_sum, returned, own, *parts):
    own[...] = near_sum[0] + returned[0].astype(jnp.float32)
    for by, part in enumerate(parts, 1):
        part[...] = (near_sum[by] + returned[by].astype(jnp.float32)).astype(jnp.bfloat16)


def combine(near_sum, returned):
    blocks, tokens, features = near_sum.shape
    whole = pl.BlockSpec(memory_space=pltpu.VMEM)
    return pl.pallas_call(
        combine_kernel,
        out_shape=(jax.ShapeDtypeStruct((tokens, features), jnp.float32),)
        + (jax.ShapeDtypeStruct((tokens, features), jnp.bfloat16),) * (blocks - 1),
        in_specs=[whole] * 2,
        out_specs=[whole] * blocks,
        compiler_params=pltpu.CompilerParams(vmem_limit_bytes=8 * 1024 * 1024),
        name="combine",
    )(near_sum, returned)


def leave_kernel(step, counts, *refs):
    outs = len(counts) + 2
    fresh, results, both, first = refs[-outs - 1], refs[-outs:-2], refs[-2], refs[-1]
    is_last = lax.axis_index("section") == lax.axis_size("section") - 1
    at = 0
    for micro, out in enumerate(results):
        inflow, *parts = refs[at : at + counts[micro]]
        at += counts[micro]
        total = inflow[...].astype(jnp.float32)
        for part in parts:
            total = total + part[...].reshape(out.shape).astype(jnp.float32)
        result = total.astype(jnp.bfloat16)
        out[...] = result
        arrived = fresh[step, micro].astype(jnp.float32)
        gone = jnp.where(is_last, arrived, result.astype(jnp.float32)).astype(jnp.bfloat16)
        both[micro] = gone
        if micro == 0:
            first[...] = gone


def leave(step, inflows, parts, fresh):
    rows = jax.ShapeDtypeStruct(inflows[0].shape, jnp.bfloat16)
    operands, counts = [], []
    for inflow, some in zip(inflows, parts):
        operands += [inflow, *some]
        counts.append(1 + len(some))
    operands.append(fresh)
    whole = pl.BlockSpec(memory_space=pltpu.VMEM)
    return pl.pallas_call(
        functools.partial(leave_kernel, step, counts),
        out_shape=(rows,) * len(inflows)
        + (jax.ShapeDtypeStruct((len(inflows),) + rows.shape, rows.dtype), rows),
        in_specs=[whole] * len(operands),
        out_specs=[whole] * (len(inflows) + 2),
        compiler_params=pltpu.CompilerParams(vmem_limit_bytes=8 * 1024 * 1024),
        name="leave",
    )(*operands)


def swapped(value, mask):
    size = lax.axis_size("expert")
    return lax.ppermute(value, "expert", [(i, i ^ mask) for i in range(size)])


def next_section(value, by):
    sections, size = lax.axis_size("section"), lax.axis_size("expert")
    pairs = [
        (s * size + i, (s + 1) % sections * size + (i ^ 4 * by))
        for s in range(sections)
        for i in range(size)
    ]
    return lax.ppermute(value, ("section", "expert"), pairs)


def previous_section(value):
    sections = lax.axis_size("section")
    return lax.ppermute(value, "section", [(s, (s - 1) % sections) for s in range(sections)])


def serve_kernel(
    features, hidden_count, chunk, experts_all, local_count, step,
    near, far, near_tail, far_tail, gain, own_in, far_in, own_out, far_out,
    near_sum, far_sum, rows, hidden,
):
    blocks, tokens = near.shape[:2]
    half = blocks * tokens
    for start, part in ((0, near), (half, far)):
        for block in range(blocks):
            at = start + block * tokens
            rows[at : at + tokens] = normalize(part[block, :, :features], gain[...])
    tail = jnp.concatenate(
        [part[:, :, features:].reshape(half, -1) for part in (near_tail, far_tail)]
    ).astype(jnp.float32)
    lane = lax.broadcasted_iota(jnp.int32, tail.shape, 1) - 2 * experts_all * step
    me = lax.axis_index("expert")
    total = None
    for side, (w_in, w_out) in enumerate(((own_in, own_out), (far_in, far_out))):
        for own in range(local_count):
            which = (me + side * (1 - 2 * (me % 2))) * local_count + own
            chosen = (lane == which) | (lane == which + experts_all)
            weight = jnp.sum(jnp.where(chosen, tail, 0.0), axis=-1, keepdims=True)
            for at in range(0, hidden_count, chunk):
                gate = jnp.dot(
                    rows[...], w_in[own, :, pl.ds(at, chunk)], preferred_element_type=jnp.float32
                )
                up = jnp.dot(
                    rows[...],
                    w_in[own, :, pl.ds(hidden_count + at, chunk)],
                    preferred_element_type=jnp.float32,
                )
                value = gate / (1.0 + jnp.exp(-gate)) * up * weight
                hidden[:, pl.ds(at, chunk)] = value.astype(jnp.bfloat16)
            out = jnp.dot(hidden[...], w_out[own], preferred_element_type=jnp.float32)
            total = out if total is None else total + out
    near_sum[...] = total[:half].reshape(near_sum.shape)
    far_sum[...] = total[half:].astype(jnp.bfloat16).reshape(far_sum.shape)


def serve(step, near, far, near_tail, far_tail, gain, own_in, far_in, own_out, far_out, experts_all):
    blocks, tokens, _ = near.shape
    local_count, features, _ = own_in.shape
    hidden_count = own_out.shape[1]
    chunk = 256 if hidden_count % 256 == 0 else hidden_count
    rows_all = 2 * blocks * tokens
    held = 2 * (own_in.size + own_out.size) * 2
    whole = pl.BlockSpec(memory_space=pltpu.VMEM)
    return pl.pallas_call(
        functools.partial(
            serve_kernel, features, hidden_count, chunk, experts_all, local_count, step
        ),
        out_shape=(
            jax.ShapeDtypeStruct((blocks, tokens, features), jnp.float32),
            jax.ShapeDtypeStruct((blocks, tokens, features), jnp.bfloat16),
        ),
        in_specs=[whole] * 9,
        out_specs=[whole] * 2,
        scratch_shapes=[
            pltpu.VMEM((rows_all, features), jnp.bfloat16),
            pltpu.VMEM((rows_all, hidden_count), jnp.bfloat16),
        ],
        compiler_params=pltpu.CompilerParams(vmem_limit_bytes=held + 10 * 1024 * 1024),
        cost_estimate=pl.CostEstimate(
            flops=2 * rows_all * 2 * local_count * 3 * features * hidden_count,
            bytes_accessed=held,
            transcendentals=rows_all * 2 * local_count * hidden_count,
        ),
        name="serve",
    )(near, far, near_tail, far_tail, gain, own_in, far_in, own_out, far_out)


def tied(*values):
    return lax.optimization_barrier(values)


def local(in_flight, arriving, norm_gain, gate_up, w_down, expert_ids, route_weights):
    owners = lax.axis_size("expert")
    outer = owners // 4
    local_count = gate_up.shape[1]
    experts_all = owners * local_count
    steps = expert_ids.shape[0]
    micro_count = in_flight.shape[1]
    micros = range(micro_count)
    both, first = first_payloads(
        in_flight[0],
        jnp.swapaxes(expert_ids[:, 0], -1, -2),
        jnp.swapaxes(route_weights[:, 0], -1, -2),
        experts_all,
    )
    both, first, gate_up, w_down = tied(both, first, gate_up, w_down)
    own_in, own_out = gate_up[0], w_down[0]
    far_in, far_out = swapped(own_in, 1), swapped(own_out, 1)
    gain = hold(first, own_in, own_out, norm_gain)
    inflows = [in_flight[0, micro] for micro in micros]
    top = outer // 2
    masks = [4 * bit for bit in (1 << place for place in range(outer.bit_length())) if bit < outer]
    masks = masks[-2:0:-1] + [2] + masks[:1] * (len(masks) > 1)
    tails = [None] * micro_count
    outputs = []
    for step in range(steps):
        if step == 0:
            here = both
            there = swapped(both, 4 * top)
            blocks = {by: swapped(first, 4 * by) for by in range(outer - 1, 0, -1) if by != top}
        else:
            there = next_section(both, top)
            blocks = {by: next_section(first, by) for by in range(outer - 1, 0, -1) if by != top}
            here = next_section(both, 0)
            inflows = [here[micro] for micro in micros]
        near, far = [], []
        here, there, *others = tied(here, there, *blocks.values())
        blocks = dict(zip(blocks, others))
        if step == 0:
            there, gain = tied(there, gain)
        for micro in micros:
            if micro == 0:
                blocks[0], blocks[top] = here[0], there[0]
                value = jnp.stack([blocks[by] for by in range(outer)])
                last = 2
            else:
                value = jnp.stack([here[micro], there[micro]])
                for mask in masks[:-1]:
                    value = jnp.concatenate([value, swapped(value, mask)])
                last = masks[-1]
            near.append(value)
            far.append(swapped(value, last))
        if step == 0:
            tails = list(zip(near, far))
        sums, sent = [], []
        for micro in micros:
            if micro > 0:
                far[micro], sums[micro - 1] = tied(far[micro], sums[micro - 1])
            one_sum, one_sent = serve(
                step, near[micro], far[micro], *tails[micro], gain,
                own_in, far_in, own_out, far_out, experts_all,
            )
            sums.append(one_sum)
            sent.append(one_sent)
        parts = []
        for micro in micros:
            own, *sends = combine(sums[micro], swapped(sent[micro], 2 if micro == 0 else masks[-1]))
            returned = []
            for number in range(len(sends), 0, -1):
                if micro == 0:
                    mask = 4 * number
                else:
                    mask = 0
                    for place, step_mask in enumerate([4 * top] + masks[:-1]):
                        mask ^= step_mask * (number >> place & 1)
                returned.append(swapped(sends[number - 1], mask))
            parts.append([own, *returned])
        if step < steps - 1:
            *results, both, first = leave(step, inflows, parts, arriving)
        else:
            results = []
            for micro in micros:
                total = inflows[micro].astype(jnp.float32)
                for part in parts[micro]:
                    total = total + part.reshape(total.shape).astype(jnp.float32)
                results.append(total.astype(jnp.bfloat16))
        outputs.append(jnp.stack(results))
    return jnp.stack(outputs)[:, None]


def solution(mesh):
    return jax.shard_map(
        local,
        mesh=mesh,
        in_specs=(
            P("section", None, "expert", None),
            P(None, None, "expert", None),
            P("section", None),
            P("section", "expert", None, None),
            P("section", "expert", None, None),
            P(None, "section", None, "expert", None),
            P(None, "section", None, "expert", None),
        ),
        out_specs=P(None, "section", None, "expert", None),
        check_vma=False,
    )
```

```python
import functools

import jax
import jax.numpy as jnp
from jax import lax
from jax.experimental import pallas as pl
from jax.experimental.pallas import tpu as pltpu
from jax.sharding import PartitionSpec as P

LANES = 128


def normalize(inflow, gain_row):
    widened = inflow.astype(jnp.float32)
    inverse_rms = lax.rsqrt(jnp.mean(widened * widened, axis=-1, keepdims=True) + 1e-06)
    return (widened * inverse_rms * gain_row).astype(jnp.bfloat16)


def token_weights(experts_all, width, ids, weights):
    steps, micro_count, top_count, tokens = ids.shape
    expert = lax.broadcasted_iota(jnp.int32, (experts_all, tokens), 0)
    columns = []
    for micro in range(micro_count):
        rows = []
        for step in range(steps):
            dense = jnp.zeros((experts_all, tokens), jnp.float32)
            for k in range(top_count):
                named = ids[step, micro, k : k + 1, :] == expert
                dense = dense + jnp.where(named, weights[step, micro, k : k + 1, :], 0.0)
            high = dense.astype(jnp.bfloat16).astype(jnp.float32)
            rows += [high, dense - high]
        empty = width - 2 * steps * experts_all
        if empty > 0:
            rows.append(jnp.zeros((empty, tokens), jnp.float32))
        columns.append(jnp.concatenate(rows, axis=0))
    return jnp.concatenate(columns, axis=1).T.astype(jnp.bfloat16).reshape(
        micro_count, tokens, width
    )


def first_kernel(experts_all, inflow_hbm, ids_hbm, weights_hbm, *refs):
    both, first, inflow, ids, weights, sem = refs
    copies = [
        pltpu.make_async_copy(source, target, sem.at[number])
        for number, (source, target) in enumerate(
            ((ids_hbm, ids), (weights_hbm, weights), (inflow_hbm, inflow))
        )
    ]
    for copy in copies:
        copy.start()
    for copy in copies:
        copy.wait()
    features = inflow.shape[-1]
    tails = token_weights(experts_all, both.shape[-1] - features, ids, weights)
    both[:, :, :features] = inflow[...]
    both[:, :, features:] = tails
    first[:, :features] = inflow[0]
    first[:, features:] = tails[0]


def first_payloads(inflow, ids, weights, experts_all):
    micro_count, tokens, features = inflow.shape
    width = -(-2 * experts_all * ids.shape[0] // LANES) * LANES
    return pl.pallas_call(
        functools.partial(first_kernel, experts_all),
        out_shape=(
            jax.ShapeDtypeStruct((micro_count, tokens, features + width), jnp.bfloat16),
            jax.ShapeDtypeStruct((tokens, features + width), jnp.bfloat16),
        ),
        in_specs=[pl.BlockSpec(memory_space=pltpu.HBM)] * 3,
        out_specs=[pl.BlockSpec(memory_space=pltpu.VMEM)] * 2,
        scratch_shapes=[
            pltpu.VMEM(inflow.shape, inflow.dtype),
            pltpu.VMEM(ids.shape, ids.dtype),
            pltpu.VMEM(weights.shape, weights.dtype),
            pltpu.SemaphoreType.DMA((3,)),
        ],
        compiler_params=pltpu.CompilerParams(vmem_limit_bytes=60 * 1024 * 1024),
        name="first_payloads",
    )(inflow, ids, weights)


def hold_kernel(after, own_in, own_out, gain, kept):
    del after, own_in, own_out
    kept[...] = gain[...]


def hold(after, own_in, own_out, gain):
    whole = pl.BlockSpec(memory_space=pltpu.VMEM)
    return pl.pallas_call(
        hold_kernel,
        out_shape=jax.ShapeDtypeStruct(gain.shape, gain.dtype),
        in_specs=[pl.BlockSpec(memory_space=pl.ANY), whole, whole, whole],
        out_specs=whole,
        compiler_params=pltpu.CompilerParams(
            vmem_limit_bytes=2 * (own_in.size + own_out.size) + 8 * 1024 * 1024
        ),
        name="hold",
    )(after, own_in, own_out, gain)


def combine_kernel(near_sum, returned, own, *parts):
    own[...] = near_sum[0] + returned[0].astype(jnp.float32)
    for by, part in enumerate(parts, 1):
        part[...] = (near_sum[by] + returned[by].astype(jnp.float32)).astype(jnp.bfloat16)


def combine(near_sum, returned):
    blocks, tokens, features = near_sum.shape
    whole = pl.BlockSpec(memory_space=pltpu.VMEM)
    return pl.pallas_call(
        combine_kernel,
        out_shape=(jax.ShapeDtypeStruct((tokens, features), jnp.float32),)
        + (jax.ShapeDtypeStruct((tokens, features), jnp.bfloat16),) * (blocks - 1),
        in_specs=[whole] * 2,
        out_specs=[whole] * blocks,
        compiler_params=pltpu.CompilerParams(vmem_limit_bytes=8 * 1024 * 1024),
        name="combine",
    )(near_sum, returned)


def leave_kernel(step, counts, *refs):
    outs = len(counts) + 2
    fresh, results, both, first = refs[-outs - 1], refs[-outs:-2], refs[-2], refs[-1]
    is_last = lax.axis_index("section") == lax.axis_size("section") - 1
    at = 0
    for micro, out in enumerate(results):
        inflow, *parts = refs[at : at + counts[micro]]
        at += counts[micro]
        total = inflow[...].astype(jnp.float32)
        for part in parts:
            total = total + part[...].reshape(out.shape).astype(jnp.float32)
        result = total.astype(jnp.bfloat16)
        out[...] = result
        arrived = fresh[step, micro].astype(jnp.float32)
        gone = jnp.where(is_last, arrived, result.astype(jnp.float32)).astype(jnp.bfloat16)
        both[micro] = gone
        if micro == 0:
            first[...] = gone


def leave(step, inflows, parts, fresh):
    rows = jax.ShapeDtypeStruct(inflows[0].shape, jnp.bfloat16)
    operands, counts = [], []
    for inflow, some in zip(inflows, parts):
        operands += [inflow, *some]
        counts.append(1 + len(some))
    operands.append(fresh)
    whole = pl.BlockSpec(memory_space=pltpu.VMEM)
    return pl.pallas_call(
        functools.partial(leave_kernel, step, counts),
        out_shape=(rows,) * len(inflows)
        + (jax.ShapeDtypeStruct((len(inflows),) + rows.shape, rows.dtype), rows),
        in_specs=[whole] * len(operands),
        out_specs=[whole] * (len(inflows) + 2),
        compiler_params=pltpu.CompilerParams(vmem_limit_bytes=8 * 1024 * 1024),
        name="leave",
    )(*operands)


def swapped(value, mask):
    size = lax.axis_size("expert")
    return lax.ppermute(value, "expert", [(i, i ^ mask) for i in range(size)])


def next_section(value, by):
    sections, size = lax.axis_size("section"), lax.axis_size("expert")
    pairs = [
        (s * size + i, (s + 1) % sections * size + (i ^ 4 * by))
        for s in range(sections)
        for i in range(size)
    ]
    return lax.ppermute(value, ("section", "expert"), pairs)


def previous_section(value):
    sections = lax.axis_size("section")
    return lax.ppermute(value, "section", [(s, (s - 1) % sections) for s in range(sections)])


def serve_kernel(
    features, hidden_count, chunk, experts_all, local_count, step,
    near, far, near_tail, far_tail, gain, own_in, far_in, own_out, far_out,
    near_sum, far_sum, rows, hidden,
):
    blocks, tokens = near.shape[:2]
    half = blocks * tokens
    for start, part in ((0, near), (half, far)):
        for block in range(blocks):
            at = start + block * tokens
            rows[at : at + tokens] = normalize(part[block, :, :features], gain[...])
    tail = jnp.concatenate(
        [part[:, :, features:].reshape(half, -1) for part in (near_tail, far_tail)]
    ).astype(jnp.float32)
    lane = lax.broadcasted_iota(jnp.int32, tail.shape, 1) - 2 * experts_all * step
    me = lax.axis_index("expert")
    total = None
    for side, (w_in, w_out) in enumerate(((own_in, own_out), (far_in, far_out))):
        for own in range(local_count):
            which = (me + side * (1 - 2 * (me % 2))) * local_count + own
            chosen = (lane == which) | (lane == which + experts_all)
            weight = jnp.sum(jnp.where(chosen, tail, 0.0), axis=-1, keepdims=True)
            for at in range(0, hidden_count, chunk):
                gate = jnp.dot(
                    rows[...], w_in[own, :, pl.ds(at, chunk)], preferred_element_type=jnp.float32
                )
                up = jnp.dot(
                    rows[...],
                    w_in[own, :, pl.ds(hidden_count + at, chunk)],
                    preferred_element_type=jnp.float32,
                )
                value = gate / (1.0 + jnp.exp(-gate)) * up * weight
                hidden[:, pl.ds(at, chunk)] = value.astype(jnp.bfloat16)
            out = jnp.dot(hidden[...], w_out[own], preferred_element_type=jnp.float32)
            total = out if total is None else total + out
    near_sum[...] = total[:half].reshape(near_sum.shape)
    far_sum[...] = total[half:].astype(jnp.bfloat16).reshape(far_sum.shape)


def serve(step, near, far, near_tail, far_tail, gain, own_in, far_in, own_out, far_out, experts_all):
    blocks, tokens, _ = near.shape
    local_count, features, _ = own_in.shape
    hidden_count = own_out.shape[1]
    chunk = 256 if hidden_count % 256 == 0 else hidden_count
    rows_all = 2 * blocks * tokens
    held = 2 * (own_in.size + own_out.size) * 2
    whole = pl.BlockSpec(memory_space=pltpu.VMEM)
    return pl.pallas_call(
        functools.partial(
            serve_kernel, features, hidden_count, chunk, experts_all, local_count, step
        ),
        out_shape=(
            jax.ShapeDtypeStruct((blocks, tokens, features), jnp.float32),
            jax.ShapeDtypeStruct((blocks, tokens, features), jnp.bfloat16),
        ),
        in_specs=[whole] * 9,
        out_specs=[whole] * 2,
        scratch_shapes=[
            pltpu.VMEM((rows_all, features), jnp.bfloat16),
            pltpu.VMEM((rows_all, hidden_count), jnp.bfloat16),
        ],
        compiler_params=pltpu.CompilerParams(vmem_limit_bytes=held + 10 * 1024 * 1024),
        cost_estimate=pl.CostEstimate(
            flops=2 * rows_all * 2 * local_count * 3 * features * hidden_count,
            bytes_accessed=held,
            transcendentals=rows_all * 2 * local_count * hidden_count,
        ),
        name="serve",
    )(near, far, near_tail, far_tail, gain, own_in, far_in, own_out, far_out)


def tied(*values):
    return lax.optimization_barrier(values)


def summed(inflow, parts):
    total = inflow.astype(jnp.float32)
    for part in parts:
        total = total + part.reshape(total.shape).astype(jnp.float32)
    return total.astype(jnp.bfloat16)


def local(in_flight, arriving, norm_gain, gate_up, w_down, expert_ids, route_weights):
    owners = lax.axis_size("expert")
    outer = owners // 4
    local_count = gate_up.shape[1]
    experts_all = owners * local_count
    steps = expert_ids.shape[0]
    micro_count = in_flight.shape[1]
    micros = range(micro_count)
    both, first = first_payloads(
        in_flight[0],
        jnp.swapaxes(expert_ids[:, 0], -1, -2),
        jnp.swapaxes(route_weights[:, 0], -1, -2),
        experts_all,
    )
    both, first, gate_up, w_down = tied(both, first, gate_up, w_down)
    own_in, own_out = gate_up[0], w_down[0]
    far_in, far_out = swapped(own_in, 1), swapped(own_out, 1)
    gain = hold(first, own_in, own_out, norm_gain)
    inflows = [in_flight[0, micro] for micro in micros]
    top = outer // 2
    masks = [4 * bit for bit in (1 << place for place in range(outer.bit_length())) if bit < outer]
    masks = masks[-2:0:-1] + [2] + masks[:1] * (len(masks) > 1)
    tails = [None] * micro_count
    outputs = []
    for step in range(steps):
        if step == 0:
            here = both
            there = swapped(both, 4 * top)
            blocks = {by: swapped(first, 4 * by) for by in range(outer - 1, 0, -1) if by != top}
        else:
            there = next_section(both, top)
            blocks = {by: next_section(first, by) for by in range(outer - 1, 0, -1) if by != top}
            here = next_section(both, 0)
            inflows = [here[micro] for micro in micros]
        near, far = [], []
        here, there, *others = tied(here, there, *blocks.values())
        blocks = dict(zip(blocks, others))
        if step == 0:
            there, gain = tied(there, gain)
        for micro in micros:
            if micro == 0:
                blocks[0], blocks[top] = here[0], there[0]
                value = jnp.stack([blocks[by] for by in range(outer)])
                last = 2
            else:
                value = jnp.stack([here[micro], there[micro]])
                for mask in masks[:-1]:
                    value = jnp.concatenate([value, swapped(value, mask)])
                last = masks[-1]
            near.append(value)
            far.append(swapped(value, last))
        if step == 0:
            tails = list(zip(near, far))
        sums, sent = [], []
        for micro in micros:
            if micro > 0:
                far[micro], sums[micro - 1] = tied(far[micro], sums[micro - 1])
            one_sum, one_sent = serve(
                step, near[micro], far[micro], *tails[micro], gain,
                own_in, far_in, own_out, far_out, experts_all,
            )
            sums.append(one_sum)
            sent.append(one_sent)
        parts = []
        for micro in micros:
            back = swapped(sent[micro], 2 if micro == 0 else masks[-1])
            if micro > 0:
                back, parts[micro - 1][0] = tied(back, parts[micro - 1][0])
            own, *sends = combine(sums[micro], back)
            returned = []
            for number in range(len(sends), 0, -1):
                if micro == 0:
                    mask = 4 * number
                else:
                    mask = 0
                    for place, step_mask in enumerate([4 * top] + masks[:-1]):
                        mask ^= step_mask * (number >> place & 1)
                returned.append(swapped(sends[number - 1], mask))
            parts.append([own, *returned])
        if step < steps - 1:
            inflows[0], parts[0] = summed(inflows[0], parts[0]), []
            *results, both, first = leave(step, inflows, parts, arriving)
        else:
            results = [summed(inflows[micro], parts[micro]) for micro in micros]
        outputs.append(jnp.stack(results))
    return jnp.stack(outputs)[:, None]


def solution(mesh):
    return jax.shard_map(
        local,
        mesh=mesh,
        in_specs=(
            P("section", None, "expert", None),
            P(None, None, "expert", None),
            P("section", None),
            P("section", "expert", None, None),
            P("section", "expert", None, None),
            P(None, "section", None, "expert", None),
            P(None, "section", None, "expert", None),
        ),
        out_specs=P(None, "section", None, "expert", None),
        check_vma=False,
    )
```

```python
import functools

import jax
import jax.numpy as jnp
from jax import lax
from jax.experimental import pallas as pl
from jax.experimental.pallas import tpu as pltpu
from jax.sharding import PartitionSpec as P

LANES = 128


def normalize(inflow, gain_row):
    widened = inflow.astype(jnp.float32)
    inverse_rms = lax.rsqrt(jnp.mean(widened * widened, axis=-1, keepdims=True) + 1e-06)
    return (widened * inverse_rms * gain_row).astype(jnp.bfloat16)


def token_weights(experts_all, width, ids, weights):
    steps, micro_count, top_count, tokens = ids.shape
    expert = lax.broadcasted_iota(jnp.int32, (experts_all, tokens), 0)
    columns = []
    for micro in range(micro_count):
        rows = []
        for step in range(steps):
            dense = jnp.zeros((experts_all, tokens), jnp.float32)
            for k in range(top_count):
                named = ids[step, micro, k : k + 1, :] == expert
                dense = dense + jnp.where(named, weights[step, micro, k : k + 1, :], 0.0)
            high = dense.astype(jnp.bfloat16).astype(jnp.float32)
            rows += [high, dense - high]
        empty = width - 2 * steps * experts_all
        if empty > 0:
            rows.append(jnp.zeros((empty, tokens), jnp.float32))
        columns.append(jnp.concatenate(rows, axis=0))
    return jnp.concatenate(columns, axis=1).T.astype(jnp.bfloat16).reshape(
        micro_count, tokens, width
    )


def first_kernel(experts_all, inflow_hbm, ids_hbm, weights_hbm, *refs):
    both, inflow, ids, weights, sem = refs
    copies = [
        pltpu.make_async_copy(source, target, sem.at[number])
        for number, (source, target) in enumerate(
            ((ids_hbm, ids), (weights_hbm, weights), (inflow_hbm, inflow))
        )
    ]
    for copy in copies:
        copy.start()
    for copy in copies:
        copy.wait()
    features = inflow.shape[-1]
    both[:, :, :features] = inflow[...]
    both[:, :, features:] = token_weights(experts_all, both.shape[-1] - features, ids, weights)


def first_payloads(inflow, ids, weights, experts_all):
    micro_count, tokens, features = inflow.shape
    width = -(-2 * experts_all * ids.shape[0] // LANES) * LANES
    return pl.pallas_call(
        functools.partial(first_kernel, experts_all),
        out_shape=jax.ShapeDtypeStruct((micro_count, tokens, features + width), jnp.bfloat16),
        in_specs=[pl.BlockSpec(memory_space=pltpu.HBM)] * 3,
        out_specs=pl.BlockSpec(memory_space=pltpu.VMEM),
        scratch_shapes=[
            pltpu.VMEM(inflow.shape, inflow.dtype),
            pltpu.VMEM(ids.shape, ids.dtype),
            pltpu.VMEM(weights.shape, weights.dtype),
            pltpu.SemaphoreType.DMA((3,)),
        ],
        compiler_params=pltpu.CompilerParams(vmem_limit_bytes=60 * 1024 * 1024),
        name="first_payloads",
    )(inflow, ids, weights)


def hold_kernel(after, own_in, own_out, gain, kept):
    del after, own_in, own_out
    kept[...] = gain[...]


def hold(after, own_in, own_out, gain):
    whole = pl.BlockSpec(memory_space=pltpu.VMEM)
    return pl.pallas_call(
        hold_kernel,
        out_shape=jax.ShapeDtypeStruct(gain.shape, gain.dtype),
        in_specs=[pl.BlockSpec(memory_space=pl.ANY), whole, whole, whole],
        out_specs=whole,
        compiler_params=pltpu.CompilerParams(
            vmem_limit_bytes=2 * (own_in.size + own_out.size) + 8 * 1024 * 1024
        ),
        name="hold",
    )(after, own_in, own_out, gain)


def combine_kernel(near_sum, returned, own, *parts):
    own[...] = near_sum[0] + returned[0].astype(jnp.float32)
    for by, part in enumerate(parts, 1):
        part[...] = (near_sum[by] + returned[by].astype(jnp.float32)).astype(jnp.bfloat16)


def combine(near_sum, returned):
    blocks, tokens, features = near_sum.shape
    whole = pl.BlockSpec(memory_space=pltpu.VMEM)
    return pl.pallas_call(
        combine_kernel,
        out_shape=(jax.ShapeDtypeStruct((tokens, features), jnp.float32),)
        + (jax.ShapeDtypeStruct((tokens, features), jnp.bfloat16),) * (blocks - 1),
        in_specs=[whole] * 2,
        out_specs=[whole] * blocks,
        compiler_params=pltpu.CompilerParams(vmem_limit_bytes=8 * 1024 * 1024),
        name="combine",
    )(near_sum, returned)


def leave_kernel(step, micro_count, *refs):
    fresh, leaving = refs[-2 - micro_count], refs[-1]
    results = refs[-1 - micro_count : -1]
    each = (len(refs) - 2 - micro_count) // micro_count
    is_last = lax.axis_index("section") == lax.axis_size("section") - 1
    for micro, out in enumerate(results):
        inflow, own, *parts = refs[micro * each : (micro + 1) * each]
        total = inflow[...].astype(jnp.float32) + own[...]
        for part in parts:
            total = total + part[...].astype(jnp.float32)
        result = total.astype(jnp.bfloat16)
        out[...] = result
        arrived = fresh[step, micro].astype(jnp.float32)
        gone = jnp.where(is_last, arrived, result.astype(jnp.float32))
        leaving[micro] = gone.astype(jnp.bfloat16)


def leave(step, inflows, own, parts, fresh):
    micro_count = len(own)
    rows = jax.ShapeDtypeStruct(own[0].shape, jnp.bfloat16)
    operands = []
    for micro in range(micro_count):
        operands += [inflows[micro], own[micro], *parts[micro]]
    operands.append(fresh)
    whole = pl.BlockSpec(memory_space=pltpu.VMEM)
    return pl.pallas_call(
        functools.partial(leave_kernel, step, micro_count),
        out_shape=(rows,) * micro_count
        + (jax.ShapeDtypeStruct((micro_count,) + rows.shape, rows.dtype),),
        in_specs=[whole] * len(operands),
        out_specs=[whole] * (micro_count + 1),
        compiler_params=pltpu.CompilerParams(vmem_limit_bytes=8 * 1024 * 1024),
        name="leave",
    )(*operands)


def swap_core(value):
    size = lax.axis_size("expert")
    return lax.ppermute(value, "expert", [(i, i ^ 1) for i in range(size)])


def swap_inner(value):
    size = lax.axis_size("expert")
    return lax.ppermute(value, "expert", [(i, i ^ 2) for i in range(size)])


def swap_outer(value, by):
    size = lax.axis_size("expert")
    return lax.ppermute(value, "expert", [(i, i ^ 4 * by) for i in range(size)])


def next_section(value, by):
    sections, size = lax.axis_size("section"), lax.axis_size("expert")
    pairs = [
        (s * size + i, (s + 1) % sections * size + (i ^ 4 * by))
        for s in range(sections)
        for i in range(size)
    ]
    return lax.ppermute(value, ("section", "expert"), pairs)


def previous_section(value):
    sections = lax.axis_size("section")
    return lax.ppermute(value, "section", [(s, (s - 1) % sections) for s in range(sections)])


def serve_kernel(
    features, hidden_count, chunk, experts_all, local_count, step,
    near, far, near_tail, far_tail, gain, own_in, far_in, own_out, far_out,
    near_sum, far_sum, rows, hidden,
):
    blocks, tokens = near.shape[:2]
    half = blocks * tokens
    for start, part in ((0, near), (half, far)):
        for block in range(blocks):
            at = start + block * tokens
            rows[at : at + tokens] = normalize(part[block, :, :features], gain[...])
    tail = jnp.concatenate(
        [part[:, :, features:].reshape(half, -1) for part in (near_tail, far_tail)]
    ).astype(jnp.float32)
    lane = lax.broadcasted_iota(jnp.int32, tail.shape, 1) - 2 * experts_all * step
    me = lax.axis_index("expert")
    total = None
    for side, (w_in, w_out) in enumerate(((own_in, own_out), (far_in, far_out))):
        for own in range(local_count):
            which = (me + side * (1 - 2 * (me % 2))) * local_count + own
            chosen = (lane == which) | (lane == which + experts_all)
            weight = jnp.sum(jnp.where(chosen, tail, 0.0), axis=-1, keepdims=True)
            for at in range(0, hidden_count, chunk):
                gate = jnp.dot(
                    rows[...], w_in[own, :, pl.ds(at, chunk)], preferred_element_type=jnp.float32
                )
                up = jnp.dot(
                    rows[...],
                    w_in[own, :, pl.ds(hidden_count + at, chunk)],
                    preferred_element_type=jnp.float32,
                )
                value = gate / (1.0 + jnp.exp(-gate)) * up * weight
                hidden[:, pl.ds(at, chunk)] = value.astype(jnp.bfloat16)
            out = jnp.dot(hidden[...], w_out[own], preferred_element_type=jnp.float32)
            total = out if total is None else total + out
    near_sum[...] = total[:half].reshape(near_sum.shape)
    far_sum[...] = total[half:].astype(jnp.bfloat16).reshape(far_sum.shape)


def serve(step, near, far, near_tail, far_tail, gain, own_in, far_in, own_out, far_out, experts_all):
    blocks, tokens, _ = near.shape
    local_count, features, _ = own_in.shape
    hidden_count = own_out.shape[1]
    chunk = 256 if hidden_count % 256 == 0 else hidden_count
    rows_all = 2 * blocks * tokens
    held = 2 * (own_in.size + own_out.size) * 2
    whole = pl.BlockSpec(memory_space=pltpu.VMEM)
    return pl.pallas_call(
        functools.partial(
            serve_kernel, features, hidden_count, chunk, experts_all, local_count, step
        ),
        out_shape=(
            jax.ShapeDtypeStruct((blocks, tokens, features), jnp.float32),
            jax.ShapeDtypeStruct((blocks, tokens, features), jnp.bfloat16),
        ),
        in_specs=[whole] * 9,
        out_specs=[whole] * 2,
        scratch_shapes=[
            pltpu.VMEM((rows_all, features), jnp.bfloat16),
            pltpu.VMEM((rows_all, hidden_count), jnp.bfloat16),
        ],
        compiler_params=pltpu.CompilerParams(vmem_limit_bytes=held + 10 * 1024 * 1024),
        cost_estimate=pl.CostEstimate(
            flops=2 * rows_all * 2 * local_count * 3 * features * hidden_count,
            bytes_accessed=held,
            transcendentals=rows_all * 2 * local_count * hidden_count,
        ),
        name="serve",
    )(near, far, near_tail, far_tail, gain, own_in, far_in, own_out, far_out)


def tied(*values):
    return lax.optimization_barrier(values)


def local(in_flight, arriving, norm_gain, gate_up, w_down, expert_ids, route_weights):
    owners = lax.axis_size("expert")
    outer = owners // 4
    local_count = gate_up.shape[1]
    experts_all = owners * local_count
    steps = expert_ids.shape[0]
    micro_count = in_flight.shape[1]
    micros = range(micro_count)
    both = first_payloads(
        in_flight[0],
        jnp.swapaxes(expert_ids[:, 0], -1, -2),
        jnp.swapaxes(route_weights[:, 0], -1, -2),
        experts_all,
    )
    both, gate_up, w_down = tied(both, gate_up, w_down)
    own_in, own_out = gate_up[0], w_down[0]
    far_in, far_out = swap_core(own_in), swap_core(own_out)
    gain = norm_gain
    inflows = [in_flight[0, micro] for micro in micros]
    outputs = []
    for step in range(steps):
        near, far, own, parts, results = [], [], [], [], []
        if step == 0:
            hopped = [swap_outer(both, by) for by in range(outer - 1, 0, -1)] + [both]
        else:
            hopped = [next_section(leaving, by) for by in range(outer - 1, -1, -1)]
        for micro in micros:
            blocks = [block[micro] for block in hopped]
            if step > 0:
                inflows[micro] = blocks[-1]
            near.append(jnp.stack(blocks[::-1]))
            if step == 0 and micro == 0:
                gain = hold(both, own_in, own_out, gain)
                near[0], gain = tied(near[0], gain)
            far.append(swap_inner(near[micro]))
        if step == 0:
            near_tail, far_tail = near, far
        returned = []
        for micro in micros:
            near_sum, far_sum = serve(
                step, near[micro], far[micro], near_tail[micro], far_tail[micro], gain,
                own_in, far_in, own_out, far_out, experts_all,
            )
            own.append(near_sum)
            returned.append(swap_inner(far_sum))
        for micro in micros:
            own[micro], *blocks = combine(own[micro], returned[micro])
            parts.append([swap_outer(blocks[by - 1], by) for by in range(outer - 1, 0, -1)])
        if step < steps - 1:
            *results, leaving = leave(step, inflows, own, parts, arriving)
        else:
            for micro in micros:
                total = inflows[micro].astype(jnp.float32) + own[micro]
                for part in parts[micro]:
                    total = total + part.astype(jnp.float32)
                results.append(total.astype(jnp.bfloat16))
        outputs.append(jnp.stack(results))
    return jnp.stack(outputs)[:, None]


def solution(mesh):
    return jax.shard_map(
        local,
        mesh=mesh,
        in_specs=(
            P("section", None, "expert", None),
            P(None, None, "expert", None),
            P("section", None),
            P("section", "expert", None, None),
            P("section", "expert", None, None),
            P(None, "section", None, "expert", None),
            P(None, "section", None, "expert", None),
        ),
        out_specs=P(None, "section", None, "expert", None),
        check_vma=False,
    )
```
